32 devices in a mesh: xy: 16 (over z, x, core), gz: 2 (over y).
Axes of the slice: x: 2, y: 2, z: 4, core: 2. Of those that a mesh axis runs over, the one named last changes fastest.
Arguments:
- file_data: float32 [512, 64, 4096], P('gz', None, 'xy')
- factor: float32 [512, 256], P('gz'), may hold values from -0.25 to 0.25
- block_owner: int32 [32], replicated, may hold values from 0 to 15, as said below
- block_offset: int32 [32], replicated, may hold values from 0 to 128, as said below
Outputs:
- gram: float32 [512, 512], P('gz')
- core: float32 [256, 64, 4096], P('gz', None, 'xy')
The draws below stay inside these ranges and needn't reach their ends.
Inputs may be any that keep to these rules, and one draw needn't show every extreme that they name: `block_owner`: block b of device d (b = d * 2 + j) is owned by d - 1, d or d + 1 modulo 16. Every index of xy owns exactly 2 blocks. `block_offset`: offsets are multiples of 128; the blocks of one owner take distinct offsets, so every file slot is named once.
All inputs are finite; a program needn't handle non-finite values.
Results may differ from the reference program's by a relative error of at most 0.00007.
Values sent between devices are 32-bit elements; how exact they have to be, the bound alone decides.
No kernel may reach another device: no remote copies, remote signals or barrier semaphores. Data moves between devices by JAX's collectives and lax.ppermute only.
A program may use at most 128 MiB of HBM per device.

```python
import jax
import jax.numpy as jnp
from jax import lax

Z = 512
SPECIES = 64
RANK = 256
BLOCKS_DEV = 2
FILE_BLOCKS = 2
FILE_ROWS = 4096
N_XY = 16


def block_tables(key):
    key = jax.random.fold_in(key, 11)
    parity_key, keep_key, perm_key = jax.random.split(key, 3)
    half = N_XY // 2
    middle = N_XY // 2
    parity = jax.random.randint(parity_key, (BLOCKS_DEV,), 0, 2)
    parity = parity.at[0].set(1).at[1].set(0)
    keep = jax.random.randint(keep_key, (BLOCKS_DEV, half), 0, 2)
    column = jnp.arange(BLOCKS_DEV)[:, None]
    pair_index = jnp.arange(half)[None, :]
    first_forced = (pair_index == half - 1) | (pair_index == (middle - 2) // 2)
    second_forced = (pair_index == 0) | (pair_index == middle // 2) | (pair_index == half - 1)
    keep = jnp.where((column == 0) & first_forced, 1, keep)
    keep = jnp.where((column == 1) & second_forced, 1, keep)
    device = jnp.arange(N_XY)[:, None]
    moved = (device - parity[None, :]) % N_XY
    pair = moved // 2
    position = moved % 2
    kept = keep[jnp.arange(BLOCKS_DEV)[None, :], pair]
    sides = jnp.where(position == 0, 1, -1) * kept
    owner = ((device + sides) % N_XY).reshape(-1)
    count = owner.shape[0]
    earlier = jnp.arange(count)[None, :] < jnp.arange(count)[:, None]
    same = owner[None, :] == owner[:, None]
    ranks = jnp.sum((earlier & same).astype(jnp.int32), axis=1)
    perms = jax.vmap(lambda k: jax.random.permutation(k, FILE_BLOCKS))(jax.random.split(perm_key, N_XY))
    offset = perms[owner, ranks] * 128
    return (owner.astype(jnp.int32), offset.astype(jnp.int32))


def draw_block_owner(key, part):
    return block_tables(key)[0]


def draw_block_offset(key, part):
    return block_tables(key)[1]


def draw_file_data(key, part):
    keys = jax.random.split(key, 3)
    zscale = jnp.exp(jax.random.uniform(keys[0], (Z, 1, 1), jnp.float32, -0.7, 0.7))
    sscale = jnp.exp(jax.random.uniform(keys[1], (1, SPECIES, 1), jnp.float32, -0.7, 0.7))
    values = jax.random.normal(keys[2], (Z, SPECIES, FILE_ROWS), jnp.float32)
    return (values * zscale * sscale).astype(jnp.float32)


def steps_of(key, extent, cuts, smallest, top_value):
    gain = 1.0
    for axis_at, parts in cuts:
        heights = jax.random.uniform(jax.random.fold_in(jax.random.fold_in(key, 6), axis_at), (parts,), jnp.float32, smallest / len(cuts), top_value / len(cuts))
        gain = gain * jnp.repeat(jnp.exp(heights), extent[axis_at] // parts).reshape((-1,) + (1,) * (len(extent) - 1 - axis_at))
    return gain


def centred(key, dims, scale, most, cuts=(), kind=jnp.bfloat16):
    gain = steps_of(key, dims, cuts, -0.22, 0.18) if cuts else 1.0
    array = jax.random.normal(key, dims, jnp.float32) * scale * gain
    return jnp.minimum(jnp.maximum(array, -most), most).astype(kind)


def setup_inputs(seed: int = 0) -> dict:
    seeds = jax.random.split(jax.random.key(seed), 5)
    file_data = draw_file_data(jax.random.fold_in(seeds[4], 71), 0)
    factor = centred(seeds[1], (Z, RANK), Z ** -0.5, 0.25, ((0, 2),), jnp.float32)
    block_owner = draw_block_owner(jax.random.fold_in(seeds[4], 71), 0)
    block_offset = draw_block_offset(jax.random.fold_in(seeds[4], 71), 0)
    return {"file_data": file_data, "factor": factor, "block_owner": block_owner, "block_offset": block_offset}


def reference(file_data, factor, block_owner, block_offset):
    file_dev = file_data.shape[2] // N_XY
    starts = block_owner.astype(jnp.int32) * file_dev + block_offset.astype(jnp.int32)
    index = (starts[:, None] + jnp.arange(128, dtype=jnp.int32)[None, :]).reshape(-1)
    field = jnp.take(file_data, index, axis=2)
    scale = 1.0 / (index.shape[0] * file_data.shape[1])
    gram = jnp.einsum("zcs,wcs->zw", field, field, precision=lax.Precision.HIGHEST) * scale
    core = jnp.einsum("zr,zcs->rcs", factor, field, precision=lax.Precision.HIGHEST)
    return gram, core
```

```python
import functools

import jax
import jax.numpy as jnp
from jax import lax
from jax.experimental import pallas as pl
from jax.experimental.pallas import tpu as pltpu
from jax.sharding import PartitionSpec as P

BLOCKS_DEV = 2
POINTS = 128
TILE = 8
VMEM_LIMIT = 60 * 1024 * 1024
COST = pl.CostEstimate(flops=3 * 10**10, bytes_accessed=0, transcendentals=0)
MINE, THEIRS, CORE, SOURCE, SLOT = 0, 1, 2, 3, 3 + BLOCKS_DEV


def shifted(array, axis, by):
    length = lax.axis_size(axis)
    return lax.ppermute(array, axis, [(i, (i + by) % length) for i in range(length)])


def halves(x):
    high = x.astype(jnp.bfloat16)
    return high, (x - high.astype(jnp.float32)).astype(jnp.bfloat16)


def dot(a, b):
    return lax.dot_general(a, b, (((1,), (0,)), ((), ())), preferred_element_type=jnp.float32)


def dot_nt(a, b):
    return lax.dot_general(a, b, (((1,), (1,)), ((), ())), preferred_element_type=jnp.float32)


def dot3(a, b, kind):
    return kind(a[0], b[0]) + (kind(a[0], b[1]) + kind(a[1], b[0]))


def species(ref, s):
    rows, tile, points = ref.shape
    flat = ref.reshape(rows * tile, points)
    return jnp.concatenate([flat[pl.ds(s + k, rows, stride=tile), :] for k in range(2)], axis=1)


def put_species(ref, s, value):
    rows, tile, points = ref.shape
    flat = ref.reshape(rows * tile, points)
    for k in range(2):
        flat[pl.ds(s + k, rows, stride=tile), :] = value[:, k * points : (k + 1) * points]


class Steps:
    def __init__(self, index):
        self.index = index
        self.last = []

    def call(self, kernel, name, grid, inputs, outputs, aliases=None, scratch=()):
        held = [array for array, _ in inputs]
        extra = [a for a in self.last if not any(a is h for h in held)]
        count = len(inputs)

        def body(index_ref, *refs):
            kernel(index_ref, *refs[:count], *refs[count + len(extra) :])

        result = pl.pallas_call(
            body,
            out_shape=[jax.ShapeDtypeStruct(shape, jnp.float32) for shape, _ in outputs],
            grid_spec=pltpu.PrefetchScalarGridSpec(
                num_scalar_prefetch=1,
                grid=grid,
                in_specs=[spec for _, spec in inputs] + [pl.BlockSpec(memory_space=pl.ANY)] * len(extra),
                out_specs=[spec for _, spec in outputs],
                scratch_shapes=list(scratch),
            ),
            input_output_aliases={k + 1: v for k, v in (aliases or {}).items()},
            compiler_params=pltpu.CompilerParams(vmem_limit_bytes=VMEM_LIMIT),
            cost_estimate=COST,
            name=name,
        )(self.index, *held, *extra)
        self.last = [result[0]]
        return result


def whole(shape):
    return pl.BlockSpec(shape, lambda *args: (0,) * len(shape))


def field_chunk(z, chunks, at, i):
    return pl.BlockSpec((z, TILE, POINTS), lambda p, w: (0, w[at] * chunks + i, p))


def core_chunk(rank):
    return pl.BlockSpec((rank, TILE, POINTS), lambda p, w: (0, 0, p))


def ranks(z, rank, at):
    return pl.BlockSpec((z, rank), lambda p, w: (0, w[at]))


def staged(sources, stages, targets, in_sems, out_sems):
    loads = [pltpu.make_async_copy(a, b, in_sems.at[k]) for k, (a, b) in enumerate(zip(sources, stages))]
    stores = [pltpu.make_async_copy(a, b, out_sems.at[k]) for k, (a, b) in enumerate(zip(stages, targets))]
    for load in loads:
        load.start()
    for load, store in zip(loads, stores):
        load.wait()
        store.start()
    for store in stores:
        store.wait()


def copy_field_kernel(i, index_ref, field_ref, out_ref, stage_ref, in_sems, out_sems):
    count = in_sems.shape[0]
    slab = out_ref.shape[0] // count
    first = pl.multiple_of((index_ref[THEIRS] * (field_ref.shape[1] // (2 * TILE)) + i) * TILE, TILE)
    slabs = [pl.ds(k * slab, slab) for k in range(count)]
    staged(
        [field_ref.at[at, pl.ds(first, TILE), :] for at in slabs],
        [stage_ref.at[at] for at in slabs],
        [out_ref.at[at] for at in slabs],
        in_sems,
        out_sems,
    )


def copy_kernel(index_ref, in_ref, out_ref):
    out_ref[...] = in_ref[...]


def add_kernel(index_ref, a_ref, b_ref, out_ref):
    out_ref[...] = a_ref[...] + b_ref[...]


def core_part_kernel(index_ref, factor_ref, field_ref, out_ref):
    at = halves(factor_ref[...].T)
    for s in range(0, TILE, 2):
        put_species(out_ref, s, dot3(at, halves(species(field_ref, s)), dot))


def core_finish_kernel(index_ref, factor_ref, field_ref, arrived_ref, out_ref):
    at = halves(factor_ref[...].T)
    for s in range(0, TILE, 2):
        put_species(out_ref, s, species(arrived_ref, s) + dot3(at, halves(species(field_ref, s)), dot))


def received_kernel(
    first, last, index_ref, factor_ref, cross_factor_ref, mine_ref, theirs_ref, *rest
):
    core_ref, cross_ref = rest[-2:]
    step = pl.program_id(0)

    @pl.when(step == 0)
    def _():
        cross_ref[...] = jnp.zeros_like(cross_ref) if first else rest[0][...]

    at = halves(jnp.concatenate([factor_ref[...].T, cross_factor_ref[...].T], axis=1))
    total = cross_ref[...]
    for s in range(0, TILE, 2):
        mine = halves(species(mine_ref, s))
        theirs = halves(species(theirs_ref, s))
        total = total + dot3(mine, theirs, dot_nt)
        both = tuple(jnp.concatenate([m, t], axis=0) for m, t in zip(mine, theirs))
        put_species(core_ref, s, dot3(at, both, dot))
    cross_ref[...] = total

    if last:
        @pl.when((step == pl.num_programs(0) - 1) & (index_ref[MINE] == 1))
        def _():
            cross_ref[...] = cross_ref[...].T


def diagonal_kernel(scale, index_ref, field_ref, keep_ref, send_ref, high_ref, mixed_ref):
    step = pl.program_id(0)

    @pl.when(step == 0)
    def _():
        high_ref[...] = jnp.zeros_like(high_ref)
        mixed_ref[...] = jnp.zeros_like(mixed_ref)

    high_sum, mixed_sum = high_ref[...], mixed_ref[...]
    for s in range(0, TILE, 2):
        high, low = halves(species(field_ref, s))
        high_sum = high_sum + dot_nt(high, high)
        mixed_sum = mixed_sum + dot_nt(high, low)
    high_ref[...] = high_sum
    mixed_ref[...] = mixed_sum

    @pl.when(step == pl.num_programs(0) - 1)
    def _():
        mixed = mixed_ref[...]
        high_ref[...] = (high_ref[...] + (mixed + mixed.T)) * scale
        half = keep_ref.shape[0]
        odd = index_ref[CORE]
        keep_ref[...] = high_ref[pl.ds(pl.multiple_of(odd * half, half), half), :]
        send_ref[...] = high_ref[pl.ds(pl.multiple_of((1 - odd) * half, half), half), :]


def sum_kernel(scale, index_ref, pieces_ref, out_ref):
    total = jnp.sum(pieces_ref[...], axis=0) * scale
    out_ref[...] = jnp.broadcast_to(total[None], out_ref.shape)


def gram_kernel(index_ref, diagonal_ref, cross_ref, out_ref):
    z = cross_ref.shape[0]

    @pl.when(index_ref[MINE] == 0)
    def _():
        out_ref[:, :z] = diagonal_ref[...]
        out_ref[:, z:] = cross_ref[...]

    @pl.when(index_ref[MINE] == 1)
    def _():
        out_ref[:, :z] = cross_ref[...].T
        out_ref[:, z:] = diagonal_ref[...]


def place_kernel(index_ref, here_ref, lower_ref, upper_ref, *rest):
    out_ref = rest[-1]
    source = index_ref[SOURCE + pl.program_id(0)]

    @pl.when(source == 0)
    def _():
        out_ref[...] = here_ref[...]

    @pl.when(source == 1)
    def _():
        out_ref[...] = lower_ref[...]

    @pl.when(source == 2)
    def _():
        out_ref[...] = upper_ref[...]


def put_kernel(i, index_ref, part_ref, old_ref, core_ref, stage_ref, in_sems, out_sems):
    count = in_sems.shape[0]
    slab = part_ref.shape[0] // count
    first = pl.multiple_of((index_ref[THEIRS] * (core_ref.shape[1] // (2 * TILE)) + i) * TILE, TILE)
    staged(
        [part_ref.at[pl.ds(k * slab, slab)] for k in range(count)],
        [stage_ref.at[pl.ds(k * slab, slab)] for k in range(count)],
        [core_ref.at[pl.ds(k * slab, slab), pl.ds(first, TILE), :] for k in range(count)],
        in_sems,
        out_sems,
    )


def join_kernel(axis, index_ref, keep_ref, other_ref, out_ref):
    half = keep_ref.shape[axis]
    odd = index_ref[CORE]
    for value_ref, first in ((keep_ref, odd * half), (other_ref, (1 - odd) * half)):
        part = pl.ds(pl.multiple_of(first, half), half)
        out_ref[(part, slice(None)) if axis == 0 else (slice(None), part)] = value_ref[...]


def block_sources(block_owner, block_offset):
    devices = lax.axis_size("xy")
    myself = lax.axis_index("xy")
    owner = lax.dynamic_slice_in_dim(block_owner, myself * BLOCKS_DEV, BLOCKS_DEV)
    offset = lax.dynamic_slice_in_dim(block_offset, myself * BLOCKS_DEV, BLOCKS_DEV)
    lower = (myself + devices - 1) % devices
    source = jnp.where(owner == myself, 0, jnp.where(owner == lower, 1, 2))
    return source.astype(jnp.int32), (offset // POINTS).astype(jnp.int32)


def local_pair(field, factor, block_owner, block_offset):
    z, count, points = field.shape
    mine = lax.axis_index("gz")
    group = count // 2
    rank = factor.shape[1] // 2
    chunks = group // TILE
    columns = points // POINTS
    scale = 1.0 / (count * points * lax.axis_size("xy"))
    source, slot = block_sources(block_owner, block_offset)
    along = lax.axis_index("xy")
    places = jnp.stack([mine, 1 - mine, along % 2]).astype(jnp.int32)
    steps = Steps(jnp.concatenate([places, source, slot]))
    any_space = pl.BlockSpec(memory_space=pl.ANY)
    whole_factor = whole(factor.shape)
    slabs = 4

    def staging(rows):
        return [pltpu.VMEM((rows, TILE, points), jnp.float32)] + [pltpu.SemaphoreType.DMA((slabs,))] * 2

    def neighbours(part):
        return part, shifted(part, "xy", 1), shifted(part, "xy", -1)

    def over_gz(part):
        return shifted(part, "gz", 1)

    def exchanged(part, bit):
        return lax.ppermute(part, "xy", [(i, i ^ bit) for i in range(lax.axis_size("xy"))])

    def send_field(i):
        kernel = functools.partial(copy_field_kernel, i)
        out = ((z, TILE, points), any_space)
        return over_gz(steps.call(kernel, "copy", (1,), [(field, any_space)], [out], None, staging(z))[0])

    def send_factor():
        out = ((z, rank), whole((z, rank)))
        half = over_gz(steps.call(copy_kernel, "copy", (1,), [(factor, ranks(z, rank, CORE))], [out])[0])
        return half, exchanged(half, 1)

    def core_send(i):
        inputs = [(factor, ranks(z, rank, THEIRS)), (field, field_chunk(z, chunks, MINE, i))]
        out = ((rank, TILE, points), core_chunk(rank))
        return steps.call(core_part_kernel, "core_send", (columns,), inputs, [out])[0]

    def core_finish(i, arrived):
        inputs = [
            (factor, ranks(z, rank, MINE)),
            (field, field_chunk(z, chunks, THEIRS, i)),
            (arrived, core_chunk(rank)),
        ]
        out = ((rank, TILE, points), core_chunk(rank))
        return steps.call(core_finish_kernel, "core_finish", (columns,), inputs, [out])[0]

    def received(i, theirs, cross_factor, cross, both):
        out_rank = 2 * rank if both else rank
        factor_spec = whole_factor if both else ranks(z, rank, MINE)
        inputs = [
            (factor, factor_spec),
            (cross_factor, factor_spec),
            (field, field_chunk(z, chunks, MINE, i)),
            (theirs, pl.BlockSpec((z, TILE, POINTS), lambda p, w: (0, 0, p))),
        ]
        if cross is not None:
            inputs.append((cross, whole((z, z))))
        outputs = [((out_rank, TILE, points), core_chunk(out_rank)), ((z, z), whole((z, z)))]
        kernel = functools.partial(received_kernel, cross is None, i == chunks - 1)
        return steps.call(kernel, "received", (columns,), inputs, outputs)

    def diagonal_gram():
        block = pl.BlockSpec((z, TILE, POINTS), lambda i, w: (0, i // columns, i % columns))
        scratch = [pltpu.VMEM((z, z), jnp.float32)] * 2
        grid = (count // TILE * columns,)
        half = ((z // 2, z), whole((z // 2, z)))
        kernel = functools.partial(diagonal_kernel, scale)
        return steps.call(kernel, "diagonal", grid, [(field, block)], [half, half], None, scratch)

    def small(kernel, *arrays):
        spec = whole(arrays[0].shape)
        return steps.call(kernel, "small", (1,), [(a, spec) for a in arrays], [(arrays[0].shape, spec)])[0]

    def joined(axis, keep, other):
        spec = whole(keep.shape)
        shape = tuple(n * 2 if k == axis else n for k, n in enumerate(keep.shape))
        kernel = functools.partial(join_kernel, axis)
        return steps.call(kernel, "join", (1,), [(keep, spec), (other, spec)], [(shape, whole(shape))])[0]

    def spread(matrix, axes):
        parts = lax.axis_size(axes)
        pieces = matrix.reshape(parts, z // parts, z)
        return lax.all_to_all(pieces, axes, split_axis=0, concat_axis=0, tiled=True)

    def summed(pieces, axes):
        spec = whole(pieces.shape)
        kernel = functools.partial(sum_kernel, scale)
        total = steps.call(kernel, "sum", (1,), [(pieces, spec)], [(pieces.shape, spec)])[0]
        return lax.all_to_all(total, axes, split_axis=0, concat_axis=0, tiled=True).reshape(z, z)

    def place(parts, half=None, core=None, at=MINE, i=0):
        rows = (lambda w: 0) if half is None else (lambda w: w[half])
        spec = pl.BlockSpec((rank, TILE, POINTS), lambda j, w: (rows(w), 0, w[SLOT + j]))
        inputs = [(part, spec) for part in parts]
        if core is None:
            return steps.call(place_kernel, "place", (BLOCKS_DEV,), inputs, [((rank, TILE, points), core_chunk(rank))])[0]
        out = ((rank, count, points), field_chunk(rank, chunks, at, i))
        if core is EMPTY:
            return steps.call(place_kernel, "place", (BLOCKS_DEV,), inputs, [out])[0]
        inputs.append((core, any_space))
        return steps.call(place_kernel, "place", (BLOCKS_DEV,), inputs, [out], {3: 0})[0]

    def put(part, core, i):
        out = ((rank, count, points), any_space)
        kernel = functools.partial(put_kernel, i)
        inputs = [(part, any_space), (core, any_space)]
        return steps.call(kernel, "put", (1,), inputs, [out], {1: 0}, staging(rank))[0]

    fields, ready, arrived = {}, {}, {}
    arrived[2] = over_gz(core_send(2))
    cross_half = send_factor()
    fields[0] = send_field(0)
    diagonal, half = diagonal_gram()
    half = exchanged(half, 1)
    fields[1] = send_field(1)
    diagonal = small(add_kernel, diagonal, half)
    half = exchanged(diagonal, 2)
    cross_factor = joined(1, *cross_half)
    diagonal = small(add_kernel, diagonal, half)
    half = exchanged(diagonal, 4)
    late2 = neighbours(core_finish(2, arrived[2]))
    diagonal = small(add_kernel, diagonal, half)
    half = exchanged(diagonal, 8)
    core = place(late2, None, EMPTY, THEIRS, 2)
    diagonal = small(add_kernel, diagonal, half)
    half = exchanged(diagonal, 1)
    part, cross = received(0, fields[0], cross_factor, None, True)
    ready[0] = neighbours(part)
    diagonal = joined(0, diagonal, half)
    fields[2] = send_field(2)
    part, cross = received(1, fields[1], cross_factor, cross, True)
    ready[1] = neighbours(part)
    core = place(ready[0], MINE, core, MINE, 0)
    fields[3] = send_field(3)
    part, cross = received(2, fields[2], cross_factor, cross, False)
    ready[2] = neighbours(part)
    core = place(ready[1], MINE, core, MINE, 1)
    arrived[3] = over_gz(core_send(3))
    core = place(ready[2], None, core, MINE, 2)
    part, cross = received(3, fields[3], cross_factor, cross, False)
    ready[3] = neighbours(part)
    cross = spread(cross, ("xy", "gz"))
    arrived[0] = over_gz(place(ready[0], THEIRS))
    late3 = neighbours(core_finish(3, arrived[3]))
    cross = summed(cross, ("xy", "gz"))
    core = place(ready[3], None, core, MINE, 3)
    arrived[1] = over_gz(place(ready[1], THEIRS))
    core = put(arrived[0], core, 0)
    gram_specs = [(diagonal, whole((z, z))), (cross, whole((z, z)))]
    gram = steps.call(gram_kernel, "gram", (1,), gram_specs, [((z, 2 * z), whole((z, 2 * z)))])[0]
    core = place(late3, None, core, THEIRS, 3)
    core = put(arrived[1], core, 1)
    return (gram, core)


EMPTY = object()


def local_many(field, factor, block_owner, block_offset):
    parts = lax.axis_size("gz")
    mine = lax.axis_index("gz")
    z, count, points = field.shape
    scale = 1.0 / (count * points * lax.axis_size("xy"))
    swapped = lax.all_to_all(field, "gz", split_axis=1, concat_axis=0, tiled=True)
    part = jnp.einsum("zcs,wcs->zw", swapped, swapped, precision=lax.Precision.HIGHEST)
    rows = lax.psum_scatter(part, "gz", scatter_dimension=0, tiled=True)
    gram = lax.psum(rows, "xy") * scale
    whole_factor = lax.all_gather(factor, "gz", axis=0, tiled=True)
    core_part = jnp.einsum("zr,zcs->rcs", whole_factor, swapped, precision=lax.Precision.HIGHEST)
    core = lax.all_to_all(core_part, "gz", split_axis=0, concat_axis=1, tiled=True)
    source, slot = block_sources(block_owner, block_offset)
    stack = (core, shifted(core, "xy", 1), shifted(core, "xy", -1))
    blocks = []
    for j in range(BLOCKS_DEV):
        here, lower, upper = (lax.dynamic_slice_in_dim(a, slot[j] * POINTS, POINTS, 2) for a in stack)
        blocks.append(jnp.where(source[j] == 0, here, jnp.where(source[j] == 1, lower, upper)))
    return (gram, jnp.concatenate(blocks, axis=2))


def solution(mesh):
    return jax.shard_map(
        local_pair if mesh.shape["gz"] == 2 else local_many,
        mesh=mesh,
        in_specs=(P("gz", None, "xy"), P("gz", None), P(), P()),
        out_specs=(P("gz", None), P("gz", None, "xy")),
        check_vma=False,
    )
```

```python
import functools

import jax
import jax.numpy as jnp
from jax import lax
from jax.experimental import pallas as pl
from jax.experimental.pallas import tpu as pltpu
from jax.sharding import PartitionSpec as P

BLOCKS_DEV = 2
POINTS = 128
TILE = 8
VMEM_LIMIT = 60 * 1024 * 1024
HEAVY = 3 * 10**10
WEIGHTS = {15: 0.3, 16: 0.3, 19: 0, 21: 0, 22: 0, 26: 0, 28: 0.1, 29: 0.1, 30: 3, 31: 3, 32: 3}
MINE, THEIRS, CORE, SOURCE, SLOT = 0, 1, 2, 3, 3 + BLOCKS_DEV


def shifted(array, axis, by):
    length = lax.axis_size(axis)
    return lax.ppermute(array, axis, [(i, (i + by) % length) for i in range(length)])


def halves(x):
    high = x.astype(jnp.bfloat16)
    return high, (x - high.astype(jnp.float32)).astype(jnp.bfloat16)


def dot(a, b):
    return lax.dot_general(a, b, (((1,), (0,)), ((), ())), preferred_element_type=jnp.float32)


def dot_nt(a, b):
    return lax.dot_general(a, b, (((1,), (1,)), ((), ())), preferred_element_type=jnp.float32)


def dot3(a, b, kind):
    return kind(a[0], b[0]) + (kind(a[0], b[1]) + kind(a[1], b[0]))


def species(ref, s):
    rows, tile, points = ref.shape
    flat = ref.reshape(rows * tile, points)
    return jnp.concatenate([flat[pl.ds(s + k, rows, stride=tile), :] for k in range(2)], axis=1)


def put_species(ref, s, value):
    rows, tile, points = ref.shape
    flat = ref.reshape(rows * tile, points)
    for k in range(2):
        flat[pl.ds(s + k, rows, stride=tile), :] = value[:, k * points : (k + 1) * points]


class Steps:
    def __init__(self, index):
        self.index = index
        self.last = []
        self.count = 0

    def call(self, kernel, name, grid, inputs, outputs, aliases=None, scratch=(), index=None):
        weight = WEIGHTS.get(self.count, 1)
        self.count += 1
        held = [array for array, _ in inputs]
        extra = [a for a in self.last if not any(a is h for h in held)]
        count = len(inputs)

        def body(index_ref, *refs):
            kernel(index_ref, *refs[:count], *refs[count + len(extra) :])

        result = pl.pallas_call(
            body,
            out_shape=[jax.ShapeDtypeStruct(shape, jnp.float32) for shape, _ in outputs],
            grid_spec=pltpu.PrefetchScalarGridSpec(
                num_scalar_prefetch=1,
                grid=grid,
                in_specs=[spec for _, spec in inputs] + [pl.BlockSpec(memory_space=pl.ANY)] * len(extra),
                out_specs=[spec for _, spec in outputs],
                scratch_shapes=list(scratch),
            ),
            input_output_aliases={k + 1: v for k, v in (aliases or {}).items()},
            compiler_params=pltpu.CompilerParams(vmem_limit_bytes=VMEM_LIMIT),
            cost_estimate=pl.CostEstimate(flops=int(HEAVY * weight), bytes_accessed=0, transcendentals=0),
            name=name,
        )(self.index if index is None else index, *held, *extra)
        self.last = [result[0]]
        return result


def whole(shape):
    return pl.BlockSpec(shape, lambda *args: (0,) * len(shape))


def field_chunk(z, chunks, at, i):
    return pl.BlockSpec((z, TILE, POINTS), lambda p, w: (0, w[at] * chunks + i, p))


def core_chunk(rank):
    return pl.BlockSpec((rank, TILE, POINTS), lambda p, w: (0, 0, p))


def ranks(z, rank, at):
    return pl.BlockSpec((z, rank), lambda p, w: (0, w[at]))


def staged(sources, stages, targets, in_sems, out_sems):
    loads = [pltpu.make_async_copy(a, b, in_sems.at[k]) for k, (a, b) in enumerate(zip(sources, stages))]
    stores = [pltpu.make_async_copy(a, b, out_sems.at[k]) for k, (a, b) in enumerate(zip(stages, targets))]
    for load in loads:
        load.start()
    for load, store in zip(loads, stores):
        load.wait()
        store.start()
    for store in stores:
        store.wait()


def copy_field_kernel(i, index_ref, field_ref, out_ref, stage_ref, in_sems, out_sems):
    count = in_sems.shape[0]
    slab = out_ref.shape[0] // count
    first = pl.multiple_of((index_ref[THEIRS] * (field_ref.shape[1] // (2 * TILE)) + i) * TILE, TILE)
    slabs = [pl.ds(k * slab, slab) for k in range(count)]
    staged(
        [field_ref.at[at, pl.ds(first, TILE), :] for at in slabs],
        [stage_ref.at[at] for at in slabs],
        [out_ref.at[at] for at in slabs],
        in_sems,
        out_sems,
    )


def copy_kernel(index_ref, in_ref, out_ref):
    out_ref[...] = in_ref[...]


def add_kernel(index_ref, a_ref, b_ref, out_ref):
    out_ref[...] = a_ref[...] + b_ref[...]


def core_part_kernel(index_ref, factor_ref, field_ref, out_ref):
    at = halves(factor_ref[...].T)
    for s in range(0, TILE, 2):
        put_species(out_ref, s, dot3(at, halves(species(field_ref, s)), dot))


def core_finish_kernel(index_ref, factor_ref, field_ref, arrived_ref, out_ref):
    at = halves(factor_ref[...].T)
    for s in range(0, TILE, 2):
        put_species(out_ref, s, species(arrived_ref, s) + dot3(at, halves(species(field_ref, s)), dot))


def cross_kernel(first, last, index_ref, mine_ref, theirs_ref, *rest):
    out_ref = rest[-1]
    step = pl.program_id(0)

    @pl.when(step == 0)
    def _():
        out_ref[...] = jnp.zeros_like(out_ref) if first else rest[0][...]

    total = out_ref[...]
    for s in range(0, TILE, 2):
        total = total + dot3(halves(species(mine_ref, s)), halves(species(theirs_ref, s)), dot_nt)
    out_ref[...] = total

    if last:
        @pl.when((step == pl.num_programs(0) - 1) & (index_ref[MINE] == 1))
        def _():
            out_ref[...] = out_ref[...].T


def core_kernel(index_ref, factor_ref, cross_factor_ref, mine_ref, theirs_ref, out_ref):
    at = halves(jnp.concatenate([factor_ref[...].T, cross_factor_ref[...].T], axis=1))
    for s in range(0, TILE, 2):
        both = jnp.concatenate([species(mine_ref, s), species(theirs_ref, s)], axis=0)
        put_species(out_ref, s, dot3(at, halves(both), dot))


def received_kernel(first, index_ref, factor_ref, cross_factor_ref, mine_ref, theirs_ref, *rest):
    core_ref, cross_ref = rest[-2:]
    core_kernel(index_ref, factor_ref, cross_factor_ref, mine_ref, theirs_ref, core_ref)
    cross_kernel(first, False, index_ref, mine_ref, theirs_ref, *rest[:-2], cross_ref)


def diagonal_kernel(scale, index_ref, field_ref, keep_ref, send_ref, high_ref, mixed_ref):
    step = pl.program_id(0)

    @pl.when(step == 0)
    def _():
        high_ref[...] = jnp.zeros_like(high_ref)
        mixed_ref[...] = jnp.zeros_like(mixed_ref)

    high_sum, mixed_sum = high_ref[...], mixed_ref[...]
    for s in range(0, TILE, 2):
        high, low = halves(species(field_ref, s))
        high_sum = high_sum + dot_nt(high, high)
        mixed_sum = mixed_sum + dot_nt(high, low)
    high_ref[...] = high_sum
    mixed_ref[...] = mixed_sum

    @pl.when(step == pl.num_programs(0) - 1)
    def _():
        mixed = mixed_ref[...]
        high_ref[...] = (high_ref[...] + (mixed + mixed.T)) * scale
        half = keep_ref.shape[0]
        odd = index_ref[CORE]
        keep_ref[...] = high_ref[pl.ds(pl.multiple_of(odd * half, half), half), :]
        send_ref[...] = high_ref[pl.ds(pl.multiple_of((1 - odd) * half, half), half), :]


def sum_kernel(scale, index_ref, pieces_ref, out_ref):
    total = jnp.sum(pieces_ref[...], axis=0) * scale
    out_ref[...] = jnp.broadcast_to(total[None], out_ref.shape)


def gram_kernel(index_ref, diagonal_ref, cross_ref, out_ref):
    z = cross_ref.shape[0]

    @pl.when(index_ref[MINE] == 0)
    def _():
        out_ref[:, :z] = diagonal_ref[...]
        out_ref[:, z:] = cross_ref[...]

    @pl.when(index_ref[MINE] == 1)
    def _():
        out_ref[:, :z] = cross_ref[...].T
        out_ref[:, z:] = diagonal_ref[...]


def place_kernel(index_ref, here_ref, lower_ref, upper_ref, *rest):
    out_ref = rest[-1]
    source = index_ref[SOURCE + pl.program_id(0)]

    @pl.when(source == 0)
    def _():
        out_ref[...] = here_ref[...]

    @pl.when(source == 1)
    def _():
        out_ref[...] = lower_ref[...]

    @pl.when(source == 2)
    def _():
        out_ref[...] = upper_ref[...]


def put_kernel(i, index_ref, part_ref, old_ref, core_ref, stage_ref, in_sems, out_sems):
    count = in_sems.shape[0]
    slab = part_ref.shape[0] // count
    first = pl.multiple_of((index_ref[THEIRS] * (core_ref.shape[1] // (2 * TILE)) + i) * TILE, TILE)
    staged(
        [part_ref.at[pl.ds(k * slab, slab)] for k in range(count)],
        [stage_ref.at[pl.ds(k * slab, slab)] for k in range(count)],
        [core_ref.at[pl.ds(k * slab, slab), pl.ds(first, TILE), :] for k in range(count)],
        in_sems,
        out_sems,
    )


def join_kernel(axis, index_ref, keep_ref, other_ref, out_ref):
    half = keep_ref.shape[axis]
    odd = index_ref[CORE]
    for value_ref, first in ((keep_ref, odd * half), (other_ref, (1 - odd) * half)):
        part = pl.ds(pl.multiple_of(first, half), half)
        out_ref[(part, slice(None)) if axis == 0 else (slice(None), part)] = value_ref[...]


def block_sources(block_owner, block_offset):
    devices = lax.axis_size("xy")
    myself = lax.axis_index("xy")
    owner = lax.dynamic_slice_in_dim(block_owner, myself * BLOCKS_DEV, BLOCKS_DEV)
    offset = lax.dynamic_slice_in_dim(block_offset, myself * BLOCKS_DEV, BLOCKS_DEV)
    lower = (myself + devices - 1) % devices
    source = jnp.where(owner == myself, 0, jnp.where(owner == lower, 1, 2))
    return source.astype(jnp.int32), (offset // POINTS).astype(jnp.int32)


def local_pair(field, factor, block_owner, block_offset):
    z, count, points = field.shape
    mine = lax.axis_index("gz")
    group = count // 2
    rank = factor.shape[1] // 2
    chunks = group // TILE
    columns = points // POINTS
    scale = 1.0 / (count * points * lax.axis_size("xy"))
    source, slot = block_sources(block_owner, block_offset)
    along = lax.axis_index("xy")
    places = jnp.stack([mine, 1 - mine, along % 2]).astype(jnp.int32)
    steps = Steps(jnp.concatenate([places, source, slot]))
    any_space = pl.BlockSpec(memory_space=pl.ANY)
    whole_factor = whole(factor.shape)
    slabs = 4
    late = (2, 3)

    def staging(rows):
        return [pltpu.VMEM((rows, TILE, points), jnp.float32)] + [pltpu.SemaphoreType.DMA((slabs,))] * 2

    def neighbours(part):
        return part, shifted(part, "xy", 1), shifted(part, "xy", -1)

    def over_gz(part):
        return shifted(part, "gz", 1)

    def exchanged(part, bit):
        return lax.ppermute(part, "xy", [(i, i ^ bit) for i in range(lax.axis_size("xy"))])

    def send_field(i):
        kernel = functools.partial(copy_field_kernel, i)
        out = ((z, TILE, points), any_space)
        index = places if i == 0 else None
        return over_gz(steps.call(kernel, "copy", (1,), [(field, any_space)], [out], None, staging(z), index)[0])

    def send_factor():
        out = ((z, rank), whole((z, rank)))
        half = steps.call(copy_kernel, "copy", (1,), [(factor, ranks(z, rank, CORE))], [out], index=places)[0]
        half = over_gz(half)
        return half, exchanged(half, 1)

    def core_send(i):
        inputs = [(factor, ranks(z, rank, THEIRS)), (field, field_chunk(z, chunks, MINE, i))]
        out = ((rank, TILE, points), core_chunk(rank))
        index = places if i == late[0] else None
        return steps.call(core_part_kernel, "core_send", (columns,), inputs, [out], index=index)[0]

    def core_finish(i, arrived):
        inputs = [
            (factor, ranks(z, rank, MINE)),
            (field, field_chunk(z, chunks, THEIRS, i)),
            (arrived, core_chunk(rank)),
        ]
        out = ((rank, TILE, points), core_chunk(rank))
        return steps.call(core_finish_kernel, "core_finish", (columns,), inputs, [out])[0]

    def both_halves(i, theirs):
        received = pl.BlockSpec((z, TILE, POINTS), lambda p, w: (0, 0, p))
        return [(field, field_chunk(z, chunks, MINE, i)), (theirs, received)]

    def add_cross(i, theirs, cross):
        inputs = both_halves(i, theirs) + ([] if cross is None else [(cross, whole((z, z)))])
        kernel = functools.partial(cross_kernel, cross is None, i == chunks - 1)
        return steps.call(kernel, "cross", (columns,), inputs, [((z, z), whole((z, z)))])[0]

    def core_of(i, theirs, cross_factor, ranks_spec, out_rank):
        inputs = [(factor, ranks_spec), (cross_factor, ranks_spec)] + both_halves(i, theirs)
        out = ((out_rank, TILE, points), core_chunk(out_rank))
        return steps.call(core_kernel, "core", (columns,), inputs, [out])[0]

    def received(i, theirs, cross_factor, cross, ranks_spec, out_rank):
        inputs = [(factor, ranks_spec), (cross_factor, ranks_spec)] + both_halves(i, theirs)
        if cross is not None:
            inputs.append((cross, whole((z, z))))
        outputs = [((out_rank, TILE, points), core_chunk(out_rank)), ((z, z), whole((z, z)))]
        kernel = functools.partial(received_kernel, cross is None)
        return steps.call(kernel, "received", (columns,), inputs, outputs)

    def diagonal_gram():
        block = pl.BlockSpec((z, TILE, POINTS), lambda i, w: (0, i // columns, i % columns))
        scratch = [pltpu.VMEM((z, z), jnp.float32)] * 2
        grid = (count // TILE * columns,)
        half = ((z // 2, z), whole((z // 2, z)))
        kernel = functools.partial(diagonal_kernel, scale)
        return steps.call(kernel, "diagonal", grid, [(field, block)], [half, half], None, scratch)

    def small(kernel, *arrays):
        spec = whole(arrays[0].shape)
        return steps.call(kernel, "small", (1,), [(a, spec) for a in arrays], [(arrays[0].shape, spec)])[0]

    def joined(axis, keep, other):
        spec = whole(keep.shape)
        shape = tuple(n * 2 if k == axis else n for k, n in enumerate(keep.shape))
        kernel = functools.partial(join_kernel, axis)
        return steps.call(kernel, "join", (1,), [(keep, spec), (other, spec)], [(shape, whole(shape))])[0]

    def spread(matrix, axes):
        parts = lax.axis_size(axes)
        pieces = matrix.reshape(parts, z // parts, z)
        return lax.all_to_all(pieces, axes, split_axis=0, concat_axis=0, tiled=True)

    def summed(pieces, axes):
        spec = whole(pieces.shape)
        kernel = functools.partial(sum_kernel, scale)
        total = steps.call(kernel, "sum", (1,), [(pieces, spec)], [(pieces.shape, spec)])[0]
        return lax.all_to_all(total, axes, split_axis=0, concat_axis=0, tiled=True).reshape(z, z)

    def place(parts, half=None, core=None, at=MINE, i=0):
        rows = (lambda w: 0) if half is None else (lambda w: w[half])
        spec = pl.BlockSpec((rank, TILE, POINTS), lambda j, w: (rows(w), 0, w[SLOT + j]))
        inputs = [(part, spec) for part in parts]
        if core is None:
            out = ((rank, TILE, points), core_chunk(rank))
            return steps.call(place_kernel, "place", (BLOCKS_DEV,), inputs, [out])[0]
        out = ((rank, count, points), field_chunk(rank, chunks, at, i))
        if core is EMPTY:
            return steps.call(place_kernel, "place", (BLOCKS_DEV,), inputs, [out])[0]
        inputs.append((core, any_space))
        return steps.call(place_kernel, "place", (BLOCKS_DEV,), inputs, [out], {3: 0})[0]

    def put(part, core, i):
        out = ((rank, count, points), any_space)
        kernel = functools.partial(put_kernel, i)
        inputs = [(part, any_space), (core, any_space)]
        return steps.call(kernel, "put", (1,), inputs, [out], {1: 0}, staging(rank))[0]

    fields, ready, arrived = {}, {}, {}
    own_ranks = ranks(z, rank, MINE)
    arrived[2] = over_gz(core_send(2))
    cross_half = send_factor()
    fields[0] = send_field(0)
    diagonal, half = diagonal_gram()
    half = exchanged(half, 1)
    fields[1] = send_field(1)
    diagonal = small(add_kernel, diagonal, half)
    half = exchanged(diagonal, 2)
    cross_factor = joined(1, *cross_half)
    late2 = neighbours(core_finish(2, arrived[2]))
    diagonal = small(add_kernel, diagonal, half)
    half = exchanged(diagonal, 4)
    core = place(late2, None, EMPTY, THEIRS, 2)
    diagonal = small(add_kernel, diagonal, half)
    half = exchanged(diagonal, 8)
    part, cross = received(0, fields[0], cross_factor, None, whole_factor, 2 * rank)
    ready[0] = neighbours(part)
    diagonal = small(add_kernel, diagonal, half)
    fields[2] = send_field(2)
    part, cross = received(1, fields[1], cross_factor, cross, whole_factor, 2 * rank)
    ready[1] = neighbours(part)
    core = place(ready[0], MINE, core, MINE, 0)
    fields[3] = send_field(3)
    part, cross = received(2, fields[2], cross_factor, cross, own_ranks, rank)
    ready[2] = neighbours(part)
    core = place(ready[1], MINE, core, MINE, 1)
    diagonal = small(copy_kernel, diagonal)
    half = exchanged(diagonal, 1)
    arrived[3] = over_gz(core_send(3))
    diagonal = joined(0, diagonal, half)
    core = place(ready[2], None, core, MINE, 2)
    ready[3] = neighbours(core_of(3, fields[3], cross_factor, own_ranks, rank))
    cross = spread(add_cross(3, fields[3], cross), ("xy", "gz"))
    arrived[0] = over_gz(place(ready[0], THEIRS))
    arrived[1] = over_gz(place(ready[1], THEIRS))
    late3 = neighbours(core_finish(3, arrived[3]))
    core = place(ready[3], None, core, MINE, 3)
    cross = summed(cross, ("xy", "gz"))
    core = put(arrived[0], core, 0)
    core = place(late3, None, core, THEIRS, 3)
    core = put(arrived[1], core, 1)
    gram_specs = [(diagonal, whole((z, z))), (cross, whole((z, z)))]
    gram = steps.call(gram_kernel, "gram", (1,), gram_specs, [((z, 2 * z), whole((z, 2 * z)))])[0]
    return (gram, core)


EMPTY = object()


def local_many(field, factor, block_owner, block_offset):
    parts = lax.axis_size("gz")
    mine = lax.axis_index("gz")
    z, count, points = field.shape
    scale = 1.0 / (count * points * lax.axis_size("xy"))
    swapped = lax.all_to_all(field, "gz", split_axis=1, concat_axis=0, tiled=True)
    part = jnp.einsum("zcs,wcs->zw", swapped, swapped, precision=lax.Precision.HIGHEST)
    rows = lax.psum_scatter(part, "gz", scatter_dimension=0, tiled=True)
    gram = lax.psum(rows, "xy") * scale
    whole_factor = lax.all_gather(factor, "gz", axis=0, tiled=True)
    core_part = jnp.einsum("zr,zcs->rcs", whole_factor, swapped, precision=lax.Precision.HIGHEST)
    core = lax.all_to_all(core_part, "gz", split_axis=0, concat_axis=1, tiled=True)
    source, slot = block_sources(block_owner, block_offset)
    stack = (core, shifted(core, "xy", 1), shifted(core, "xy", -1))
    blocks = []
    for j in range(BLOCKS_DEV):
        here, lower, upper = (lax.dynamic_slice_in_dim(a, slot[j] * POINTS, POINTS, 2) for a in stack)
        blocks.append(jnp.where(source[j] == 0, here, jnp.where(source[j] == 1, lower, upper)))
    return (gram, jnp.concatenate(blocks, axis=2))


def solution(mesh):
    return jax.shard_map(
        local_pair if mesh.shape["gz"] == 2 else local_many,
        mesh=mesh,
        in_specs=(P("gz", None, "xy"), P("gz", None), P(), P()),
        out_specs=(P("gz", None), P("gz", None, "xy")),
        check_vma=False,
    )
```

```python
import functools

import jax
import jax.numpy as jnp
from jax import lax
from jax.experimental import pallas as pl
from jax.experimental.pallas import tpu as pltpu
from jax.sharding import PartitionSpec as P

BLOCKS_DEV = 2
POINTS = 128
TILE = 8
VMEM_LIMIT = 60 * 1024 * 1024
HEAVY = 3 * 10**10
WEIGHTS = {15: 0.3, 16: 0.3, 18: 0.2, 19: 0, 20: 0.2, 21: 0, 22: 0, 26: 0, 28: 0.1, 29: 0.1, 30: 3, 31: 3, 32: 3}
MINE, THEIRS, CORE, SOURCE, SLOT = 0, 1, 2, 3, 3 + BLOCKS_DEV


def shifted(array, axis, by):
    length = lax.axis_size(axis)
    return lax.ppermute(array, axis, [(i, (i + by) % length) for i in range(length)])


def halves(x):
    high = x.astype(jnp.bfloat16)
    return high, (x - high.astype(jnp.float32)).astype(jnp.bfloat16)


def dot(a, b):
    return lax.dot_general(a, b, (((1,), (0,)), ((), ())), preferred_element_type=jnp.float32)


def dot_nt(a, b):
    return lax.dot_general(a, b, (((1,), (1,)), ((), ())), preferred_element_type=jnp.float32)


def dot3(a, b, kind):
    return kind(a[0], b[0]) + (kind(a[0], b[1]) + kind(a[1], b[0]))


def species(ref, s):
    rows, tile, points = ref.shape
    flat = ref.reshape(rows * tile, points)
    return jnp.concatenate([flat[pl.ds(s + k, rows, stride=tile), :] for k in range(2)], axis=1)


def put_species(ref, s, value):
    rows, tile, points = ref.shape
    flat = ref.reshape(rows * tile, points)
    for k in range(2):
        flat[pl.ds(s + k, rows, stride=tile), :] = value[:, k * points : (k + 1) * points]


class Steps:
    def __init__(self, index):
        self.index = index
        self.last = []
        self.count = 0

    def call(self, kernel, name, grid, inputs, outputs, aliases=None, scratch=(), index=None):
        weight = WEIGHTS.get(self.count, 1)
        self.count += 1
        held = [array for array, _ in inputs]
        extra = [a for a in self.last if not any(a is h for h in held)]
        count = len(inputs)

        def body(index_ref, *refs):
            kernel(index_ref, *refs[:count], *refs[count + len(extra) :])

        result = pl.pallas_call(
            body,
            out_shape=[jax.ShapeDtypeStruct(shape, jnp.float32) for shape, _ in outputs],
            grid_spec=pltpu.PrefetchScalarGridSpec(
                num_scalar_prefetch=1,
                grid=grid,
                in_specs=[spec for _, spec in inputs] + [pl.BlockSpec(memory_space=pl.ANY)] * len(extra),
                out_specs=[spec for _, spec in outputs],
                scratch_shapes=list(scratch),
            ),
            input_output_aliases={k + 1: v for k, v in (aliases or {}).items()},
            compiler_params=pltpu.CompilerParams(vmem_limit_bytes=VMEM_LIMIT),
            cost_estimate=pl.CostEstimate(flops=int(HEAVY * weight), bytes_accessed=0, transcendentals=0),
            name=name,
        )(self.index if index is None else index, *held, *extra)
        self.last = [result[0]]
        return result


def whole(shape):
    return pl.BlockSpec(shape, lambda *args: (0,) * len(shape))


def field_chunk(z, chunks, at, i):
    return pl.BlockSpec((z, TILE, POINTS), lambda p, w: (0, w[at] * chunks + i, p))


def core_chunk(rank):
    return pl.BlockSpec((rank, TILE, POINTS), lambda p, w: (0, 0, p))


def ranks(z, rank, at):
    return pl.BlockSpec((z, rank), lambda p, w: (0, w[at]))


def staged(sources, stages, targets, in_sems, out_sems):
    loads = [pltpu.make_async_copy(a, b, in_sems.at[k]) for k, (a, b) in enumerate(zip(sources, stages))]
    stores = [pltpu.make_async_copy(a, b, out_sems.at[k]) for k, (a, b) in enumerate(zip(stages, targets))]
    for load in loads:
        load.start()
    for load, store in zip(loads, stores):
        load.wait()
        store.start()
    for store in stores:
        store.wait()


def copy_field_kernel(i, index_ref, field_ref, out_ref, stage_ref, in_sems, out_sems):
    count = in_sems.shape[0]
    slab = out_ref.shape[0] // count
    first = pl.multiple_of((index_ref[THEIRS] * (field_ref.shape[1] // (2 * TILE)) + i) * TILE, TILE)
    slabs = [pl.ds(k * slab, slab) for k in range(count)]
    staged(
        [field_ref.at[at, pl.ds(first, TILE), :] for at in slabs],
        [stage_ref.at[at] for at in slabs],
        [out_ref.at[at] for at in slabs],
        in_sems,
        out_sems,
    )


def copy_kernel(index_ref, in_ref, out_ref):
    out_ref[...] = in_ref[...]


def add_kernel(index_ref, a_ref, b_ref, out_ref):
    out_ref[...] = a_ref[...] + b_ref[...]


def core_part_kernel(index_ref, factor_ref, field_ref, out_ref):
    at = halves(factor_ref[...].T)
    for s in range(0, TILE, 2):
        put_species(out_ref, s, dot3(at, halves(species(field_ref, s)), dot))


def core_finish_kernel(index_ref, factor_ref, field_ref, arrived_ref, out_ref):
    at = halves(factor_ref[...].T)
    for s in range(0, TILE, 2):
        put_species(out_ref, s, species(arrived_ref, s) + dot3(at, halves(species(field_ref, s)), dot))


def cross_kernel(first, last, index_ref, mine_ref, theirs_ref, *rest):
    out_ref = rest[-1]
    step = pl.program_id(0)

    @pl.when(step == 0)
    def _():
        out_ref[...] = jnp.zeros_like(out_ref) if first else rest[0][...]

    total = out_ref[...]
    for s in range(0, TILE, 2):
        total = total + dot3(halves(species(mine_ref, s)), halves(species(theirs_ref, s)), dot_nt)
    out_ref[...] = total

    if last:
        @pl.when((step == pl.num_programs(0) - 1) & (index_ref[MINE] == 1))
        def _():
            out_ref[...] = out_ref[...].T


def core_kernel(index_ref, factor_ref, cross_factor_ref, mine_ref, theirs_ref, out_ref):
    at = halves(jnp.concatenate([factor_ref[...].T, cross_factor_ref[...].T], axis=1))
    for s in range(0, TILE, 2):
        both = jnp.concatenate([species(mine_ref, s), species(theirs_ref, s)], axis=0)
        put_species(out_ref, s, dot3(at, halves(both), dot))


def received_kernel(first, index_ref, factor_ref, cross_factor_ref, mine_ref, theirs_ref, *rest):
    core_ref, cross_ref = rest[-2:]
    core_kernel(index_ref, factor_ref, cross_factor_ref, mine_ref, theirs_ref, core_ref)
    cross_kernel(first, False, index_ref, mine_ref, theirs_ref, *rest[:-2], cross_ref)


def diagonal_kernel(scale, index_ref, field_ref, keep_ref, send_ref, high_ref, mixed_ref):
    step = pl.program_id(0)

    @pl.when(step == 0)
    def _():
        high_ref[...] = jnp.zeros_like(high_ref)
        mixed_ref[...] = jnp.zeros_like(mixed_ref)

    high_sum, mixed_sum = high_ref[...], mixed_ref[...]
    for s in range(0, TILE, 2):
        high, low = halves(species(field_ref, s))
        high_sum = high_sum + dot_nt(high, high)
        mixed_sum = mixed_sum + dot_nt(high, low)
    high_ref[...] = high_sum
    mixed_ref[...] = mixed_sum

    @pl.when(step == pl.num_programs(0) - 1)
    def _():
        mixed = mixed_ref[...]
        high_ref[...] = (high_ref[...] + (mixed + mixed.T)) * scale
        half = keep_ref.shape[0]
        odd = index_ref[CORE]
        keep_ref[...] = high_ref[pl.ds(pl.multiple_of(odd * half, half), half), :]
        send_ref[...] = high_ref[pl.ds(pl.multiple_of((1 - odd) * half, half), half), :]


def sum_kernel(scale, index_ref, pieces_ref, out_ref):
    total = jnp.sum(pieces_ref[...], axis=0) * scale
    out_ref[...] = jnp.broadcast_to(total[None], out_ref.shape)


def place_kernel(index_ref, here_ref, lower_ref, upper_ref, *rest):
    out_ref = rest[-1]
    source = index_ref[SOURCE + pl.program_id(0)]

    @pl.when(source == 0)
    def _():
        out_ref[...] = here_ref[...]

    @pl.when(source == 1)
    def _():
        out_ref[...] = lower_ref[...]

    @pl.when(source == 2)
    def _():
        out_ref[...] = upper_ref[...]


def put_kernel(i, index_ref, part_ref, old_ref, core_ref, stage_ref, in_sems, out_sems):
    count = in_sems.shape[0]
    slab = part_ref.shape[0] // count
    first = pl.multiple_of((index_ref[THEIRS] * (core_ref.shape[1] // (2 * TILE)) + i) * TILE, TILE)
    staged(
        [part_ref.at[pl.ds(k * slab, slab)] for k in range(count)],
        [stage_ref.at[pl.ds(k * slab, slab)] for k in range(count)],
        [core_ref.at[pl.ds(k * slab, slab), pl.ds(first, TILE), :] for k in range(count)],
        in_sems,
        out_sems,
    )


def last_kernel(
    i, index_ref, part_ref, diagonal_ref, cross_ref, old_ref, core_ref, gram_ref, *scratch
):
    stage_ref, in_sems, out_sems, diagonal_stage, cross_stage, gram_sems = scratch
    z = cross_ref.shape[0]
    mine = index_ref[MINE]
    blocks = [pl.ds(pl.multiple_of(at * z, z), z) for at in (mine, 1 - mine)]
    loads = [
        pltpu.make_async_copy(diagonal_ref, diagonal_stage, gram_sems.at[0]),
        pltpu.make_async_copy(cross_ref, cross_stage, gram_sems.at[1]),
    ]
    stores = [
        pltpu.make_async_copy(diagonal_stage, gram_ref.at[:, blocks[0]], gram_sems.at[2]),
        pltpu.make_async_copy(cross_stage, gram_ref.at[:, blocks[1]], gram_sems.at[3]),
    ]
    for load in loads:
        load.start()
    put_kernel(i, index_ref, part_ref, old_ref, core_ref, stage_ref, in_sems, out_sems)
    loads[0].wait()
    stores[0].start()
    loads[1].wait()

    @pl.when(mine == 1)
    def _():
        cross_stage[...] = cross_stage[...].T

    stores[1].start()
    for store in stores:
        store.wait()


def join_kernel(axis, index_ref, keep_ref, other_ref, out_ref):
    half = keep_ref.shape[axis]
    odd = index_ref[CORE]
    for value_ref, first in ((keep_ref, odd * half), (other_ref, (1 - odd) * half)):
        part = pl.ds(pl.multiple_of(first, half), half)
        out_ref[(part, slice(None)) if axis == 0 else (slice(None), part)] = value_ref[...]


def block_sources(block_owner, block_offset):
    devices = lax.axis_size("xy")
    myself = lax.axis_index("xy")
    owner = lax.dynamic_slice_in_dim(block_owner, myself * BLOCKS_DEV, BLOCKS_DEV)
    offset = lax.dynamic_slice_in_dim(block_offset, myself * BLOCKS_DEV, BLOCKS_DEV)
    lower = (myself + devices - 1) % devices
    source = jnp.where(owner == myself, 0, jnp.where(owner == lower, 1, 2))
    return source.astype(jnp.int32), (offset // POINTS).astype(jnp.int32)


def local_pair(field, factor, block_owner, block_offset):
    z, count, points = field.shape
    mine = lax.axis_index("gz")
    group = count // 2
    rank = factor.shape[1] // 2
    chunks = group // TILE
    columns = points // POINTS
    scale = 1.0 / (count * points * lax.axis_size("xy"))
    source, slot = block_sources(block_owner, block_offset)
    along = lax.axis_index("xy")
    places = jnp.stack([mine, 1 - mine, along % 2]).astype(jnp.int32)
    steps = Steps(jnp.concatenate([places, source, slot]))
    any_space = pl.BlockSpec(memory_space=pl.ANY)
    whole_factor = whole(factor.shape)
    slabs = 4

    def staging(rows):
        return [pltpu.VMEM((rows, TILE, points), jnp.float32)] + [pltpu.SemaphoreType.DMA((slabs,))] * 2

    def neighbours(part):
        return part, shifted(part, "xy", 1), shifted(part, "xy", -1)

    def over_gz(part):
        return shifted(part, "gz", 1)

    def exchanged(part, bit):
        return lax.ppermute(part, "xy", [(i, i ^ bit) for i in range(lax.axis_size("xy"))])

    def send_field(i):
        kernel = functools.partial(copy_field_kernel, i)
        out = ((z, TILE, points), any_space)
        index = places if i == 0 else None
        return over_gz(steps.call(kernel, "copy", (1,), [(field, any_space)], [out], None, staging(z), index)[0])

    def send_factor():
        out = ((z, rank), whole((z, rank)))
        half = steps.call(copy_kernel, "copy", (1,), [(factor, ranks(z, rank, CORE))], [out], index=places)[0]
        return over_gz(half)

    def core_send(i, index=None):
        inputs = [(factor, ranks(z, rank, THEIRS)), (field, field_chunk(z, chunks, MINE, i))]
        out = ((rank, TILE, points), core_chunk(rank))
        return steps.call(core_part_kernel, "core_send", (columns,), inputs, [out], index=index)[0]

    def core_finish(i, arrived):
        inputs = [
            (factor, ranks(z, rank, MINE)),
            (field, field_chunk(z, chunks, THEIRS, i)),
            (arrived, core_chunk(rank)),
        ]
        out = ((rank, TILE, points), core_chunk(rank))
        return steps.call(core_finish_kernel, "core_finish", (columns,), inputs, [out])[0]

    def both_halves(i, theirs):
        received = pl.BlockSpec((z, TILE, POINTS), lambda p, w: (0, 0, p))
        return [(field, field_chunk(z, chunks, MINE, i)), (theirs, received)]

    def add_cross(i, theirs, cross):
        inputs = both_halves(i, theirs) + ([] if cross is None else [(cross, whole((z, z)))])
        kernel = functools.partial(cross_kernel, cross is None, i == chunks - 1)
        return steps.call(kernel, "cross", (columns,), inputs, [((z, z), whole((z, z)))])[0]

    def core_of(i, theirs, cross_factor, ranks_spec, out_rank):
        inputs = [(factor, ranks_spec), (cross_factor, ranks_spec)] + both_halves(i, theirs)
        out = ((out_rank, TILE, points), core_chunk(out_rank))
        return steps.call(core_kernel, "core", (columns,), inputs, [out])[0]

    def received(i, theirs, cross_factor, cross, ranks_spec, out_rank):
        inputs = [(factor, ranks_spec), (cross_factor, ranks_spec)] + both_halves(i, theirs)
        if cross is not None:
            inputs.append((cross, whole((z, z))))
        outputs = [((out_rank, TILE, points), core_chunk(out_rank)), ((z, z), whole((z, z)))]
        kernel = functools.partial(received_kernel, cross is None)
        return steps.call(kernel, "received", (columns,), inputs, outputs)

    def diagonal_gram():
        block = pl.BlockSpec((z, TILE, POINTS), lambda i, w: (0, i // columns, i % columns))
        scratch = [pltpu.VMEM((z, z), jnp.float32)] * 2
        grid = (count // TILE * columns,)
        half = ((z // 2, z), whole((z // 2, z)))
        kernel = functools.partial(diagonal_kernel, scale)
        return steps.call(kernel, "diagonal", grid, [(field, block)], [half, half], None, scratch)

    def small(kernel, *arrays):
        spec = whole(arrays[0].shape)
        return steps.call(kernel, "small", (1,), [(a, spec) for a in arrays], [(arrays[0].shape, spec)])[0]

    def joined(axis, keep, other):
        spec = whole(keep.shape)
        shape = tuple(n * 2 if k == axis else n for k, n in enumerate(keep.shape))
        kernel = functools.partial(join_kernel, axis)
        return steps.call(kernel, "join", (1,), [(keep, spec), (other, spec)], [(shape, whole(shape))])[0]

    def spread(matrix, axes):
        parts = lax.axis_size(axes)
        pieces = matrix.reshape(parts, z // parts, z)
        return lax.all_to_all(pieces, axes, split_axis=0, concat_axis=0, tiled=True)

    def summed(pieces, axes):
        spec = whole(pieces.shape)
        kernel = functools.partial(sum_kernel, scale)
        total = steps.call(kernel, "sum", (1,), [(pieces, spec)], [(pieces.shape, spec)])[0]
        return lax.all_to_all(total, axes, split_axis=0, concat_axis=0, tiled=True).reshape(z, z)

    def place(parts, half=None, core=None, at=MINE, i=0):
        rows = (lambda w: 0) if half is None else (lambda w: w[half])
        spec = pl.BlockSpec((rank, TILE, POINTS), lambda j, w: (rows(w), 0, w[SLOT + j]))
        inputs = [(part, spec) for part in parts]
        if core is None:
            out = ((rank, TILE, points), core_chunk(rank))
            return steps.call(place_kernel, "place", (BLOCKS_DEV,), inputs, [out])[0]
        out = ((rank, count, points), field_chunk(rank, chunks, at, i))
        if core is EMPTY:
            return steps.call(place_kernel, "place", (BLOCKS_DEV,), inputs, [out])[0]
        inputs.append((core, any_space))
        return steps.call(place_kernel, "place", (BLOCKS_DEV,), inputs, [out], {3: 0})[0]

    def put(part, core, i):
        out = ((rank, count, points), any_space)
        kernel = functools.partial(put_kernel, i)
        inputs = [(part, any_space), (core, any_space)]
        return steps.call(kernel, "put", (1,), inputs, [out], {1: 0}, staging(rank))[0]

    fields, ready, arrived = {}, {}, {}
    own_ranks = ranks(z, rank, MINE)
    arrived[2] = over_gz(core_send(2, places))
    factor_half = send_factor()
    other_half = exchanged(factor_half, 1)
    fields[0] = send_field(0)
    diagonal, half = diagonal_gram()
    half = exchanged(half, 1)
    fields[1] = send_field(1)
    diagonal = small(add_kernel, diagonal, half)
    half = exchanged(diagonal, 2)
    cross_factor = joined(1, factor_half, other_half)
    late2 = neighbours(core_finish(2, arrived[2]))
    diagonal = small(add_kernel, diagonal, half)
    half = exchanged(diagonal, 4)
    core = place(late2, None, EMPTY, THEIRS, 2)
    diagonal = small(add_kernel, diagonal, half)
    half = exchanged(diagonal, 8)
    part, cross = received(0, fields[0], cross_factor, None, whole_factor, 2 * rank)
    ready[0] = neighbours(part)
    diagonal = small(add_kernel, diagonal, half)
    fields[2] = send_field(2)
    part, cross = received(1, fields[1], cross_factor, cross, whole_factor, 2 * rank)
    ready[1] = neighbours(part)
    core = place(ready[0], MINE, core, MINE, 0)
    fields[3] = send_field(3)
    part, cross = received(2, fields[2], cross_factor, cross, own_ranks, rank)
    ready[2] = neighbours(part)
    core = place(ready[1], MINE, core, MINE, 1)
    diagonal = small(copy_kernel, diagonal)
    half = exchanged(diagonal, 1)
    arrived[3] = over_gz(core_send(3))
    diagonal = joined(0, diagonal, half)
    core = place(ready[2], None, core, MINE, 2)
    ready[3] = neighbours(core_of(3, fields[3], cross_factor, own_ranks, rank))
    cross = spread(add_cross(3, fields[3], cross), ("xy", "gz"))
    arrived[0] = over_gz(place(ready[0], THEIRS))
    arrived[1] = over_gz(place(ready[1], THEIRS))
    late3 = neighbours(core_finish(3, arrived[3]))
    core = place(ready[3], None, core, MINE, 3)
    cross = summed(cross, ("xy", "gz"))
    core = put(arrived[0], core, 0)
    core = place(late3, None, core, THEIRS, 3)
    inputs = [(array, any_space) for array in (arrived[1], diagonal, cross, core)]
    outputs = [((rank, count, points), any_space), ((z, 2 * z), any_space)]
    scratch = staging(rank) + [pltpu.VMEM((z, z), jnp.float32)] * 2 + [pltpu.SemaphoreType.DMA((4,))]
    kernel = functools.partial(last_kernel, 1)
    core, gram = steps.call(kernel, "last", (1,), inputs, outputs, {3: 0}, scratch)
    return (gram, core)


EMPTY = object()


def local_many(field, factor, block_owner, block_offset):
    parts = lax.axis_size("gz")
    mine = lax.axis_index("gz")
    z, count, points = field.shape
    scale = 1.0 / (count * points * lax.axis_size("xy"))
    swapped = lax.all_to_all(field, "gz", split_axis=1, concat_axis=0, tiled=True)
    part = jnp.einsum("zcs,wcs->zw", swapped, swapped, precision=lax.Precision.HIGHEST)
    rows = lax.psum_scatter(part, "gz", scatter_dimension=0, tiled=True)
    gram = lax.psum(rows, "xy") * scale
    whole_factor = lax.all_gather(factor, "gz", axis=0, tiled=True)
    core_part = jnp.einsum("zr,zcs->rcs", whole_factor, swapped, precision=lax.Precision.HIGHEST)
    core = lax.all_to_all(core_part, "gz", split_axis=0, concat_axis=1, tiled=True)
    source, slot = block_sources(block_owner, block_offset)
    stack = (core, shifted(core, "xy", 1), shifted(core, "xy", -1))
    blocks = []
    for j in range(BLOCKS_DEV):
        here, lower, upper = (lax.dynamic_slice_in_dim(a, slot[j] * POINTS, POINTS, 2) for a in stack)
        blocks.append(jnp.where(source[j] == 0, here, jnp.where(source[j] == 1, lower, upper)))
    return (gram, jnp.concatenate(blocks, axis=2))


def solution(mesh):
    return jax.shard_map(
        local_pair if mesh.shape["gz"] == 2 else local_many,
        mesh=mesh,
        in_specs=(P("gz", None, "xy"), P("gz", None), P(), P()),
        out_specs=(P("gz", None), P("gz", None, "xy")),
        check_vma=False,
    )
```

```python
import functools

import jax
import jax.numpy as jnp
from jax import lax
from jax.experimental import pallas as pl
from jax.experimental.pallas import tpu as pltpu
from jax.sharding import PartitionSpec as P

BLOCKS_DEV = 2
POINTS = 128
TILE = 8
VMEM_LIMIT = 60 * 1024 * 1024
HEAVY = 3 * 10**10
WEIGHTS = {15: 0.3, 16: 0.3, 18: 0.2, 19: 0, 20: 0.2, 21: 0, 22: 0, 27: 0, 29: 0.1, 30: 0.1, 31: 3, 32: 3, 33: 3}
MINE, THEIRS, CORE, SOURCE, SLOT = 0, 1, 2, 3, 3 + BLOCKS_DEV


def shifted(array, axis, by):
    length = lax.axis_size(axis)
    return lax.ppermute(array, axis, [(i, (i + by) % length) for i in range(length)])


def halves(x):
    high = x.astype(jnp.bfloat16)
    return high, (x - high.astype(jnp.float32)).astype(jnp.bfloat16)


def dot(a, b):
    return lax.dot_general(a, b, (((1,), (0,)), ((), ())), preferred_element_type=jnp.float32)


def dot_nt(a, b):
    return lax.dot_general(a, b, (((1,), (1,)), ((), ())), preferred_element_type=jnp.float32)


def dot3(a, b, kind):
    return kind(a[0], b[0]) + (kind(a[0], b[1]) + kind(a[1], b[0]))


def species(ref, s):
    rows, tile, points = ref.shape
    flat = ref.reshape(rows * tile, points)
    return jnp.concatenate([flat[pl.ds(s + k, rows, stride=tile), :] for k in range(2)], axis=1)


def put_species(ref, s, value):
    rows, tile, points = ref.shape
    flat = ref.reshape(rows * tile, points)
    for k in range(2):
        flat[pl.ds(s + k, rows, stride=tile), :] = value[:, k * points : (k + 1) * points]


class Steps:
    def __init__(self, index):
        self.index = index
        self.last = []
        self.count = 0

    def call(self, kernel, name, grid, inputs, outputs, aliases=None, scratch=(), index=None):
        weight = WEIGHTS.get(self.count, 1)
        self.count += 1
        held = [array for array, _ in inputs]
        extra = [a for a in self.last if not any(a is h for h in held)]
        count = len(inputs)

        def body(index_ref, *refs):
            kernel(index_ref, *refs[:count], *refs[count + len(extra) :])

        result = pl.pallas_call(
            body,
            out_shape=[jax.ShapeDtypeStruct(shape, jnp.float32) for shape, _ in outputs],
            grid_spec=pltpu.PrefetchScalarGridSpec(
                num_scalar_prefetch=1,
                grid=grid,
                in_specs=[spec for _, spec in inputs] + [pl.BlockSpec(memory_space=pl.ANY)] * len(extra),
                out_specs=[spec for _, spec in outputs],
                scratch_shapes=list(scratch),
            ),
            input_output_aliases={k + 1: v for k, v in (aliases or {}).items()},
            compiler_params=pltpu.CompilerParams(vmem_limit_bytes=VMEM_LIMIT),
            cost_estimate=pl.CostEstimate(flops=int(HEAVY * weight), bytes_accessed=0, transcendentals=0),
            name=name,
        )(self.index if index is None else index, *held, *extra)
        self.last = [result[0]]
        return result


def whole(shape):
    return pl.BlockSpec(shape, lambda *args: (0,) * len(shape))


def field_chunk(z, chunks, at, i):
    return pl.BlockSpec((z, TILE, POINTS), lambda p, w: (0, w[at] * chunks + i, p))


def core_chunk(rank):
    return pl.BlockSpec((rank, TILE, POINTS), lambda p, w: (0, 0, p))


def ranks(z, rank, at):
    return pl.BlockSpec((z, rank), lambda p, w: (0, w[at]))


def staged(sources, stages, targets, in_sems, out_sems):
    loads = [pltpu.make_async_copy(a, b, in_sems.at[k]) for k, (a, b) in enumerate(zip(sources, stages))]
    stores = [pltpu.make_async_copy(a, b, out_sems.at[k]) for k, (a, b) in enumerate(zip(stages, targets))]
    for load in loads:
        load.start()
    for load, store in zip(loads, stores):
        load.wait()
        store.start()
    for store in stores:
        store.wait()


def copy_field_kernel(i, index_ref, field_ref, out_ref, stage_ref, in_sems, out_sems):
    count = in_sems.shape[0]
    slab = out_ref.shape[0] // count
    first = pl.multiple_of((index_ref[THEIRS] * (field_ref.shape[1] // (2 * TILE)) + i) * TILE, TILE)
    slabs = [pl.ds(k * slab, slab) for k in range(count)]
    staged(
        [field_ref.at[at, pl.ds(first, TILE), :] for at in slabs],
        [stage_ref.at[at] for at in slabs],
        [out_ref.at[at] for at in slabs],
        in_sems,
        out_sems,
    )


def copy_kernel(index_ref, in_ref, out_ref):
    out_ref[...] = in_ref[...]


def add_kernel(index_ref, a_ref, b_ref, out_ref):
    out_ref[...] = a_ref[...] + b_ref[...]


def core_part_kernel(index_ref, factor_ref, field_ref, out_ref):
    at = halves(factor_ref[...].T)
    for s in range(0, TILE, 2):
        put_species(out_ref, s, dot3(at, halves(species(field_ref, s)), dot))


def core_finish_kernel(index_ref, factor_ref, field_ref, arrived_ref, out_ref):
    at = halves(factor_ref[...].T)
    for s in range(0, TILE, 2):
        put_species(out_ref, s, species(arrived_ref, s) + dot3(at, halves(species(field_ref, s)), dot))


def cross_kernel(first, index_ref, mine_ref, theirs_ref, *rest):
    out_ref = rest[-1]
    step = pl.program_id(0)

    @pl.when(step == 0)
    def _():
        out_ref[...] = jnp.zeros_like(out_ref) if first else rest[0][...]

    total = out_ref[...]
    for s in range(0, TILE, 2):
        total = total + dot3(halves(species(mine_ref, s)), halves(species(theirs_ref, s)), dot_nt)
    out_ref[...] = total


def cross_last_kernel(index_ref, mine_ref, theirs_ref, sum_ref, keep_ref, send_ref, total_ref):
    cross_kernel(False, index_ref, mine_ref, theirs_ref, sum_ref, total_ref)

    @pl.when(pl.program_id(0) == pl.num_programs(0) - 1)
    def _():
        @pl.when(index_ref[MINE] == 1)
        def _():
            total_ref[...] = total_ref[...].T

        half = keep_ref.shape[0]
        odd = index_ref[CORE]
        keep_ref[...] = total_ref[pl.ds(pl.multiple_of(odd * half, half), half), :]
        send_ref[...] = total_ref[pl.ds(pl.multiple_of((1 - odd) * half, half), half), :]


def core_kernel(index_ref, factor_ref, cross_factor_ref, mine_ref, theirs_ref, out_ref):
    at = halves(jnp.concatenate([factor_ref[...].T, cross_factor_ref[...].T], axis=1))
    for s in range(0, TILE, 2):
        both = jnp.concatenate([species(mine_ref, s), species(theirs_ref, s)], axis=0)
        put_species(out_ref, s, dot3(at, halves(both), dot))


def received_kernel(first, index_ref, factor_ref, cross_factor_ref, mine_ref, theirs_ref, *rest):
    core_ref, cross_ref = rest[-2:]
    core_kernel(index_ref, factor_ref, cross_factor_ref, mine_ref, theirs_ref, core_ref)
    cross_kernel(first, index_ref, mine_ref, theirs_ref, *rest[:-2], cross_ref)


def diagonal_kernel(scale, index_ref, field_ref, keep_ref, send_ref, high_ref, mixed_ref):
    step = pl.program_id(0)

    @pl.when(step == 0)
    def _():
        high_ref[...] = jnp.zeros_like(high_ref)
        mixed_ref[...] = jnp.zeros_like(mixed_ref)

    high_sum, mixed_sum = high_ref[...], mixed_ref[...]
    for s in range(0, TILE, 2):
        high, low = halves(species(field_ref, s))
        high_sum = high_sum + dot_nt(high, high)
        mixed_sum = mixed_sum + dot_nt(high, low)
    high_ref[...] = high_sum
    mixed_ref[...] = mixed_sum

    @pl.when(step == pl.num_programs(0) - 1)
    def _():
        mixed = mixed_ref[...]
        high_ref[...] = (high_ref[...] + (mixed + mixed.T)) * scale
        half = keep_ref.shape[0]
        odd = index_ref[CORE]
        keep_ref[...] = high_ref[pl.ds(pl.multiple_of(odd * half, half), half), :]
        send_ref[...] = high_ref[pl.ds(pl.multiple_of((1 - odd) * half, half), half), :]


def tiles(count, rows, columns):
    across = columns // POINTS
    high = rows * across // count
    return [(t, slice(t // across * high, (t // across + 1) * high), slice(t % across * POINTS, (t % across + 1) * POINTS)) for t in range(count)]


def cut_kernel(index_ref, keep_ref, other_ref, out_ref):
    for t, rows, columns in tiles(out_ref.shape[0], *keep_ref.shape):
        out_ref[t] = keep_ref[rows, columns] + other_ref[rows, columns]


def sum_kernel(scale, index_ref, pieces_ref, out_ref):
    count, high, _ = pieces_ref.shape
    for odd in range(2):
        total = functools.reduce(jnp.add, [pieces_ref[s] for s in range(count) if s // 2 % 2 == odd]) * scale
        out_ref[:, odd * high : (odd + 1) * high, :] = jnp.broadcast_to(total[None], (count,) + total.shape)


def place_kernel(index_ref, here_ref, lower_ref, upper_ref, *rest):
    out_ref = rest[-1]
    source = index_ref[SOURCE + pl.program_id(0)]

    @pl.when(source == 0)
    def _():
        out_ref[...] = here_ref[...]

    @pl.when(source == 1)
    def _():
        out_ref[...] = lower_ref[...]

    @pl.when(source == 2)
    def _():
        out_ref[...] = upper_ref[...]


def put_kernel(i, index_ref, part_ref, old_ref, core_ref, stage_ref, in_sems, out_sems):
    count = in_sems.shape[0]
    slab = part_ref.shape[0] // count
    first = pl.multiple_of((index_ref[THEIRS] * (core_ref.shape[1] // (2 * TILE)) + i) * TILE, TILE)
    staged(
        [part_ref.at[pl.ds(k * slab, slab)] for k in range(count)],
        [stage_ref.at[pl.ds(k * slab, slab)] for k in range(count)],
        [core_ref.at[pl.ds(k * slab, slab), pl.ds(first, TILE), :] for k in range(count)],
        in_sems,
        out_sems,
    )


def last_kernel(
    i, index_ref, part_ref, diagonal_ref, cross_ref, old_ref, core_ref, gram_ref, *scratch
):
    stage_ref, in_sems, out_sems, diagonal_stage, cross_stage, pieces_stage, gram_sems = scratch
    z = diagonal_ref.shape[0]
    mine = index_ref[MINE]
    blocks = [pl.ds(pl.multiple_of(at * z, z), z) for at in (mine, 1 - mine)]
    loads = [
        pltpu.make_async_copy(diagonal_ref, diagonal_stage, gram_sems.at[0]),
        pltpu.make_async_copy(cross_ref, pieces_stage, gram_sems.at[1]),
    ]
    stores = [
        pltpu.make_async_copy(diagonal_stage, gram_ref.at[:, blocks[0]], gram_sems.at[2]),
        pltpu.make_async_copy(cross_stage, gram_ref.at[:, blocks[1]], gram_sems.at[3]),
    ]
    for load in loads:
        load.start()
    put_kernel(i, index_ref, part_ref, old_ref, core_ref, stage_ref, in_sems, out_sems)
    loads[0].wait()
    stores[0].start()
    loads[1].wait()
    count, high, _ = pieces_stage.shape
    for odd in range(2):
        for t, rows, columns in tiles(count, z // 2, z):
            place = slice(odd * z // 2 + rows.start, odd * z // 2 + rows.stop)
            cross_stage[place, columns] = pieces_stage[t, odd * high // 2 : (odd + 1) * high // 2, :]

    @pl.when(mine == 1)
    def _():
        cross_stage[...] = cross_stage[...].T

    stores[1].start()
    for store in stores:
        store.wait()


def join_kernel(axis, index_ref, keep_ref, other_ref, out_ref):
    half = keep_ref.shape[axis]
    odd = index_ref[CORE]
    for value_ref, first in ((keep_ref, odd * half), (other_ref, (1 - odd) * half)):
        part = pl.ds(pl.multiple_of(first, half), half)
        out_ref[(part, slice(None)) if axis == 0 else (slice(None), part)] = value_ref[...]


def block_sources(block_owner, block_offset):
    devices = lax.axis_size("xy")
    myself = lax.axis_index("xy")
    owner = lax.dynamic_slice_in_dim(block_owner, myself * BLOCKS_DEV, BLOCKS_DEV)
    offset = lax.dynamic_slice_in_dim(block_offset, myself * BLOCKS_DEV, BLOCKS_DEV)
    lower = (myself + devices - 1) % devices
    source = jnp.where(owner == myself, 0, jnp.where(owner == lower, 1, 2))
    return source.astype(jnp.int32), (offset // POINTS).astype(jnp.int32)


def local_pair(field, factor, block_owner, block_offset):
    z, count, points = field.shape
    mine = lax.axis_index("gz")
    group = count // 2
    rank = factor.shape[1] // 2
    chunks = group // TILE
    columns = points // POINTS
    scale = 1.0 / (count * points * lax.axis_size("xy"))
    source, slot = block_sources(block_owner, block_offset)
    along = lax.axis_index("xy")
    places = jnp.stack([mine, 1 - mine, along % 2]).astype(jnp.int32)
    steps = Steps(jnp.concatenate([places, source, slot]))
    any_space = pl.BlockSpec(memory_space=pl.ANY)
    whole_factor = whole(factor.shape)
    slabs = 4
    axes = ("xy", "gz")

    def staging(rows):
        return [pltpu.VMEM((rows, TILE, points), jnp.float32)] + [pltpu.SemaphoreType.DMA((slabs,))] * 2

    def neighbours(part):
        return part, shifted(part, "xy", 1), shifted(part, "xy", -1)

    def over_gz(part):
        return shifted(part, "gz", 1)

    def exchanged(part, bit):
        return lax.ppermute(part, "xy", [(i, i ^ bit) for i in range(lax.axis_size("xy"))])

    def send_field(i):
        kernel = functools.partial(copy_field_kernel, i)
        out = ((z, TILE, points), any_space)
        index = places if i == 0 else None
        return over_gz(steps.call(kernel, "copy", (1,), [(field, any_space)], [out], None, staging(z), index)[0])

    def send_factor():
        out = ((z, rank), whole((z, rank)))
        half = steps.call(copy_kernel, "copy", (1,), [(factor, ranks(z, rank, CORE))], [out], index=places)[0]
        return over_gz(half)

    def core_send(i, index=None):
        inputs = [(factor, ranks(z, rank, THEIRS)), (field, field_chunk(z, chunks, MINE, i))]
        out = ((rank, TILE, points), core_chunk(rank))
        return steps.call(core_part_kernel, "core_send", (columns,), inputs, [out], index=index)[0]

    def core_finish(i, arrived):
        inputs = [
            (factor, ranks(z, rank, MINE)),
            (field, field_chunk(z, chunks, THEIRS, i)),
            (arrived, core_chunk(rank)),
        ]
        out = ((rank, TILE, points), core_chunk(rank))
        return steps.call(core_finish_kernel, "core_finish", (columns,), inputs, [out])[0]

    def both_halves(i, theirs):
        received = pl.BlockSpec((z, TILE, POINTS), lambda p, w: (0, 0, p))
        return [(field, field_chunk(z, chunks, MINE, i)), (theirs, received)]

    def add_last_cross(i, theirs, cross):
        inputs = both_halves(i, theirs) + [(cross, whole((z, z)))]
        half = ((z // 2, z), whole((z // 2, z)))
        scratch = [pltpu.VMEM((z, z), jnp.float32)]
        return steps.call(cross_last_kernel, "cross", (columns,), inputs, [half, half], None, scratch)

    def core_of(i, theirs, cross_factor, ranks_spec, out_rank):
        inputs = [(factor, ranks_spec), (cross_factor, ranks_spec)] + both_halves(i, theirs)
        out = ((out_rank, TILE, points), core_chunk(out_rank))
        return steps.call(core_kernel, "core", (columns,), inputs, [out])[0]

    def received(i, theirs, cross_factor, cross, ranks_spec, out_rank):
        inputs = [(factor, ranks_spec), (cross_factor, ranks_spec)] + both_halves(i, theirs)
        if cross is not None:
            inputs.append((cross, whole((z, z))))
        outputs = [((out_rank, TILE, points), core_chunk(out_rank)), ((z, z), whole((z, z)))]
        kernel = functools.partial(received_kernel, cross is None)
        return steps.call(kernel, "received", (columns,), inputs, outputs)

    def diagonal_gram():
        block = pl.BlockSpec((z, TILE, POINTS), lambda i, w: (0, i // columns, i % columns))
        scratch = [pltpu.VMEM((z, z), jnp.float32)] * 2
        grid = (count // TILE * columns,)
        half = ((z // 2, z), whole((z // 2, z)))
        kernel = functools.partial(diagonal_kernel, scale)
        return steps.call(kernel, "diagonal", grid, [(field, block)], [half, half], None, scratch)

    def small(kernel, *arrays):
        spec = whole(arrays[0].shape)
        return steps.call(kernel, "small", (1,), [(a, spec) for a in arrays], [(arrays[0].shape, spec)])[0]

    def joined(axis, keep, other):
        spec = whole(keep.shape)
        shape = tuple(n * 2 if k == axis else n for k, n in enumerate(keep.shape))
        kernel = functools.partial(join_kernel, axis)
        return steps.call(kernel, "join", (1,), [(keep, spec), (other, spec)], [(shape, whole(shape))])[0]

    def spread(keep, other):
        shape = (lax.axis_size(axes), z // 2 * z // lax.axis_size(axes) // POINTS, POINTS)
        inputs = [(keep, whole(keep.shape)), (other, whole(other.shape))]
        pieces = steps.call(cut_kernel, "cut", (1,), inputs, [(shape, whole(shape))])[0]
        return lax.all_to_all(pieces, axes, split_axis=0, concat_axis=0, tiled=True)

    def summed(pieces):
        count, high, _ = pieces.shape
        shape = (count, 2 * high, POINTS)
        kernel = functools.partial(sum_kernel, scale)
        total = steps.call(kernel, "sum", (1,), [(pieces, whole(pieces.shape))], [(shape, whole(shape))])[0]
        return lax.all_to_all(total, axes, split_axis=0, concat_axis=0, tiled=True)

    def place(parts, half=None, core=None, at=MINE, i=0):
        rows = (lambda w: 0) if half is None else (lambda w: w[half])
        spec = pl.BlockSpec((rank, TILE, POINTS), lambda j, w: (rows(w), 0, w[SLOT + j]))
        inputs = [(part, spec) for part in parts]
        if core is None:
            out = ((rank, TILE, points), core_chunk(rank))
            return steps.call(place_kernel, "place", (BLOCKS_DEV,), inputs, [out])[0]
        out = ((rank, count, points), field_chunk(rank, chunks, at, i))
        if core is EMPTY:
            return steps.call(place_kernel, "place", (BLOCKS_DEV,), inputs, [out])[0]
        inputs.append((core, any_space))
        return steps.call(place_kernel, "place", (BLOCKS_DEV,), inputs, [out], {3: 0})[0]

    def put(part, core, i):
        out = ((rank, count, points), any_space)
        kernel = functools.partial(put_kernel, i)
        inputs = [(part, any_space), (core, any_space)]
        return steps.call(kernel, "put", (1,), inputs, [out], {1: 0}, staging(rank))[0]

    fields, ready, arrived = {}, {}, {}
    own_ranks = ranks(z, rank, MINE)
    arrived[2] = over_gz(core_send(2, places))
    factor_half = send_factor()
    other_half = exchanged(factor_half, 1)
    fields[0] = send_field(0)
    diagonal, half = diagonal_gram()
    half = exchanged(half, 1)
    fields[1] = send_field(1)
    diagonal = small(add_kernel, diagonal, half)
    half = exchanged(diagonal, 2)
    cross_factor = joined(1, factor_half, other_half)
    late2 = neighbours(core_finish(2, arrived[2]))
    diagonal = small(add_kernel, diagonal, half)
    half = exchanged(diagonal, 4)
    core = place(late2, None, EMPTY, THEIRS, 2)
    diagonal = small(add_kernel, diagonal, half)
    half = exchanged(diagonal, 8)
    part, cross = received(0, fields[0], cross_factor, None, whole_factor, 2 * rank)
    ready[0] = neighbours(part)
    diagonal = small(add_kernel, diagonal, half)
    fields[2] = send_field(2)
    part, cross = received(1, fields[1], cross_factor, cross, whole_factor, 2 * rank)
    ready[1] = neighbours(part)
    core = place(ready[0], MINE, core, MINE, 0)
    fields[3] = send_field(3)
    part, cross = received(2, fields[2], cross_factor, cross, own_ranks, rank)
    ready[2] = neighbours(part)
    core = place(ready[1], MINE, core, MINE, 1)
    diagonal = small(copy_kernel, diagonal)
    half = exchanged(diagonal, 1)
    arrived[3] = over_gz(core_send(3))
    diagonal = joined(0, diagonal, half)
    core = place(ready[2], None, core, MINE, 2)
    ready[3] = neighbours(core_of(3, fields[3], cross_factor, own_ranks, rank))
    keep, send = add_last_cross(3, fields[3], cross)
    half = exchanged(send, 1)
    arrived[0] = over_gz(place(ready[0], THEIRS))
    cross = spread(keep, half)
    arrived[1] = over_gz(place(ready[1], THEIRS))
    late3 = neighbours(core_finish(3, arrived[3]))
    core = place(ready[3], None, core, MINE, 3)
    cross = summed(cross)
    core = put(arrived[0], core, 0)
    core = place(late3, None, core, THEIRS, 3)
    inputs = [(array, any_space) for array in (arrived[1], diagonal, cross, core)]
    outputs = [((rank, count, points), any_space), ((z, 2 * z), any_space)]
    scratch = staging(rank) + [pltpu.VMEM((z, z), jnp.float32)] * 2
    scratch += [pltpu.VMEM(cross.shape, jnp.float32), pltpu.SemaphoreType.DMA((4,))]
    kernel = functools.partial(last_kernel, 1)
    core, gram = steps.call(kernel, "last", (1,), inputs, outputs, {3: 0}, scratch)
    return (gram, core)


EMPTY = object()


def local_many(field, factor, block_owner, block_offset):
    parts = lax.axis_size("gz")
    mine = lax.axis_index("gz")
    z, count, points = field.shape
    scale = 1.0 / (count * points * lax.axis_size("xy"))
    swapped = lax.all_to_all(field, "gz", split_axis=1, concat_axis=0, tiled=True)
    part = jnp.einsum("zcs,wcs->zw", swapped, swapped, precision=lax.Precision.HIGHEST)
    rows = lax.psum_scatter(part, "gz", scatter_dimension=0, tiled=True)
    gram = lax.psum(rows, "xy") * scale
    whole_factor = lax.all_gather(factor, "gz", axis=0, tiled=True)
    core_part = jnp.einsum("zr,zcs->rcs", whole_factor, swapped, precision=lax.Precision.HIGHEST)
    core = lax.all_to_all(core_part, "gz", split_axis=0, concat_axis=1, tiled=True)
    source, slot = block_sources(block_owner, block_offset)
    stack = (core, shifted(core, "xy", 1), shifted(core, "xy", -1))
    blocks = []
    for j in range(BLOCKS_DEV):
        here, lower, upper = (lax.dynamic_slice_in_dim(a, slot[j] * POINTS, POINTS, 2) for a in stack)
        blocks.append(jnp.where(source[j] == 0, here, jnp.where(source[j] == 1, lower, upper)))
    return (gram, jnp.concatenate(blocks, axis=2))


def solution(mesh):
    return jax.shard_map(
        local_pair if mesh.shape["gz"] == 2 else local_many,
        mesh=mesh,
        in_specs=(P("gz", None, "xy"), P("gz", None), P(), P()),
        out_specs=(P("gz", None), P("gz", None, "xy")),
        check_vma=False,
    )
```

```python
import functools

import jax
import jax.numpy as jnp
from jax import lax
from jax.experimental import pallas as pl
from jax.experimental.pallas import tpu as pltpu
from jax.sharding import PartitionSpec as P

BLOCKS_DEV = 2
POINTS = 128
TILE = 8
VMEM_LIMIT = 60 * 1024 * 1024
HEAVY = 3 * 10**10
WEIGHTS = {15: 0.3, 16: 0.3, 18: 0.2, 19: 0, 20: 0.2, 21: 0, 22: 0, 27: 0, 29: 0.1, 30: 0.1, 31: 3, 32: 3, 33: 3}
MINE, THEIRS, CORE, SOURCE, SLOT = 0, 1, 2, 3, 3 + BLOCKS_DEV


def shifted(array, axis, by):
    length = lax.axis_size(axis)
    return lax.ppermute(array, axis, [(i, (i + by) % length) for i in range(length)])


def halves(x):
    high = x.astype(jnp.bfloat16)
    return high, (x - high.astype(jnp.float32)).astype(jnp.bfloat16)


def dot(a, b):
    return lax.dot_general(a, b, (((1,), (0,)), ((), ())), preferred_element_type=jnp.float32)


def dot_nt(a, b):
    return lax.dot_general(a, b, (((1,), (1,)), ((), ())), preferred_element_type=jnp.float32)


def dot3(a, b, kind):
    return kind(a[0], b[0]) + (kind(a[0], b[1]) + kind(a[1], b[0]))


def species(ref, s):
    rows, tile, points = ref.shape
    flat = ref.reshape(rows * tile, points)
    return jnp.concatenate([flat[pl.ds(s + k, rows, stride=tile), :] for k in range(2)], axis=1)


def put_species(ref, s, value):
    rows, tile, points = ref.shape
    flat = ref.reshape(rows * tile, points)
    for k in range(2):
        flat[pl.ds(s + k, rows, stride=tile), :] = value[:, k * points : (k + 1) * points]


class Steps:
    def __init__(self, index):
        self.index = index
        self.last = []
        self.count = 0

    def call(self, kernel, name, grid, inputs, outputs, aliases=None, scratch=(), index=None):
        weight = WEIGHTS.get(self.count, 1)
        self.count += 1
        held = [array for array, _ in inputs]
        extra = [a for a in self.last if not any(a is h for h in held)]
        count = len(inputs)

        def body(index_ref, *refs):
            kernel(index_ref, *refs[:count], *refs[count + len(extra) :])

        result = pl.pallas_call(
            body,
            out_shape=[jax.ShapeDtypeStruct(shape, jnp.float32) for shape, _ in outputs],
            grid_spec=pltpu.PrefetchScalarGridSpec(
                num_scalar_prefetch=1,
                grid=grid,
                in_specs=[spec for _, spec in inputs] + [pl.BlockSpec(memory_space=pl.ANY)] * len(extra),
                out_specs=[spec for _, spec in outputs],
                scratch_shapes=list(scratch),
            ),
            input_output_aliases={k + 1: v for k, v in (aliases or {}).items()},
            compiler_params=pltpu.CompilerParams(vmem_limit_bytes=VMEM_LIMIT),
            cost_estimate=pl.CostEstimate(flops=int(HEAVY * weight), bytes_accessed=0, transcendentals=0),
            name=name,
        )(self.index if index is None else index, *held, *extra)
        self.last = [result[0]]
        return result


def whole(shape):
    return pl.BlockSpec(shape, lambda *args: (0,) * len(shape))


def field_chunk(z, chunks, at, i):
    return pl.BlockSpec((z, TILE, POINTS), lambda p, w: (0, w[at] * chunks + i, p))


def core_chunk(rank):
    return pl.BlockSpec((rank, TILE, POINTS), lambda p, w: (0, 0, p))


def ranks(z, rank, at):
    return pl.BlockSpec((z, rank), lambda p, w: (0, w[at]))


def staged(sources, stages, targets, in_sems, out_sems, meanwhile=None):
    loads = [pltpu.make_async_copy(a, b, in_sems.at[k]) for k, (a, b) in enumerate(zip(sources, stages))]
    stores = [pltpu.make_async_copy(a, b, out_sems.at[k]) for k, (a, b) in enumerate(zip(stages, targets))]
    for load in loads:
        load.start()
    for load, store in zip(loads, stores):
        load.wait()
        store.start()
    if meanwhile is not None:
        meanwhile()
    for store in stores:
        store.wait()


def copy_field_kernel(i, index_ref, field_ref, out_ref, stage_ref, in_sems, out_sems):
    count = in_sems.shape[0]
    slab = out_ref.shape[0] // count
    first = pl.multiple_of((index_ref[THEIRS] * (field_ref.shape[1] // (2 * TILE)) + i) * TILE, TILE)
    slabs = [pl.ds(k * slab, slab) for k in range(count)]
    staged(
        [field_ref.at[at, pl.ds(first, TILE), :] for at in slabs],
        [stage_ref.at[at] for at in slabs],
        [out_ref.at[at] for at in slabs],
        in_sems,
        out_sems,
    )


def copy_kernel(index_ref, in_ref, out_ref):
    out_ref[...] = in_ref[...]


def add_kernel(index_ref, a_ref, b_ref, out_ref):
    out_ref[...] = a_ref[...] + b_ref[...]


def core_part_kernel(index_ref, factor_ref, field_ref, out_ref):
    at = halves(factor_ref[...].T)
    for s in range(0, TILE, 2):
        put_species(out_ref, s, dot3(at, halves(species(field_ref, s)), dot))


def core_finish_kernel(index_ref, factor_ref, field_ref, arrived_ref, out_ref):
    at = halves(factor_ref[...].T)
    for s in range(0, TILE, 2):
        put_species(out_ref, s, species(arrived_ref, s) + dot3(at, halves(species(field_ref, s)), dot))


def cross_kernel(first, index_ref, mine_ref, theirs_ref, *rest):
    out_ref = rest[-1]
    step = pl.program_id(0)

    @pl.when(step == 0)
    def _():
        out_ref[...] = jnp.zeros_like(out_ref) if first else rest[0][...]

    total = out_ref[...]
    for s in range(0, TILE, 2):
        total = total + dot3(halves(species(mine_ref, s)), halves(species(theirs_ref, s)), dot_nt)
    out_ref[...] = total


def cross_last_kernel(index_ref, mine_ref, theirs_ref, sum_ref, keep_ref, send_ref, total_ref):
    cross_kernel(False, index_ref, mine_ref, theirs_ref, sum_ref, total_ref)

    @pl.when(pl.program_id(0) == pl.num_programs(0) - 1)
    def _():
        @pl.when(index_ref[MINE] == 1)
        def _():
            total_ref[...] = total_ref[...].T

        half = keep_ref.shape[0]
        odd = index_ref[CORE]
        keep_ref[...] = total_ref[pl.ds(pl.multiple_of(odd * half, half), half), :]
        send_ref[...] = total_ref[pl.ds(pl.multiple_of((1 - odd) * half, half), half), :]


def core_kernel(index_ref, factor_ref, cross_factor_ref, mine_ref, theirs_ref, out_ref):
    at = halves(jnp.concatenate([factor_ref[...].T, cross_factor_ref[...].T], axis=1))
    for s in range(0, TILE, 2):
        both = jnp.concatenate([species(mine_ref, s), species(theirs_ref, s)], axis=0)
        put_species(out_ref, s, dot3(at, halves(both), dot))


def received_kernel(first, index_ref, factor_ref, cross_factor_ref, mine_ref, theirs_ref, *rest):
    core_ref, cross_ref = rest[-2:]
    core_kernel(index_ref, factor_ref, cross_factor_ref, mine_ref, theirs_ref, core_ref)
    cross_kernel(first, index_ref, mine_ref, theirs_ref, *rest[:-2], cross_ref)


def diagonal_kernel(scale, index_ref, field_ref, keep_ref, send_ref, high_ref, mixed_ref):
    step = pl.program_id(0)

    @pl.when(step == 0)
    def _():
        high_ref[...] = jnp.zeros_like(high_ref)
        mixed_ref[...] = jnp.zeros_like(mixed_ref)

    high_sum, mixed_sum = high_ref[...], mixed_ref[...]
    for s in range(0, TILE, 2):
        high, low = halves(species(field_ref, s))
        high_sum = high_sum + dot_nt(high, high)
        mixed_sum = mixed_sum + dot_nt(high, low)
    high_ref[...] = high_sum
    mixed_ref[...] = mixed_sum

    @pl.when(step == pl.num_programs(0) - 1)
    def _():
        mixed = mixed_ref[...]
        high_ref[...] = (high_ref[...] + (mixed + mixed.T)) * scale
        half = keep_ref.shape[0]
        odd = index_ref[CORE]
        keep_ref[...] = high_ref[pl.ds(pl.multiple_of(odd * half, half), half), :]
        send_ref[...] = high_ref[pl.ds(pl.multiple_of((1 - odd) * half, half), half), :]


def tiles(count, rows, columns):
    across = columns // POINTS
    high = rows * across // count
    return [(t, slice(t // across * high, (t // across + 1) * high), slice(t % across * POINTS, (t % across + 1) * POINTS)) for t in range(count)]


def cut_kernel(index_ref, keep_ref, other_ref, out_ref):
    for t, rows, columns in tiles(out_ref.shape[0], *keep_ref.shape):
        out_ref[t] = keep_ref[rows, columns] + other_ref[rows, columns]


def sum_kernel(scale, index_ref, pieces_ref, out_ref):
    count, high, _ = pieces_ref.shape
    for odd in range(2):
        total = functools.reduce(jnp.add, [pieces_ref[s] for s in range(count) if s // 2 % 2 == odd]) * scale
        out_ref[:, odd * high : (odd + 1) * high, :] = jnp.broadcast_to(total[None], (count,) + total.shape)


def place_kernel(index_ref, here_ref, lower_ref, upper_ref, *rest):
    out_ref = rest[-1]
    source = index_ref[SOURCE + pl.program_id(0)]

    @pl.when(source == 0)
    def _():
        out_ref[...] = here_ref[...]

    @pl.when(source == 1)
    def _():
        out_ref[...] = lower_ref[...]

    @pl.when(source == 2)
    def _():
        out_ref[...] = upper_ref[...]


def put_kernel(i, index_ref, part_ref, old_ref, core_ref, stage_ref, in_sems, out_sems, meanwhile=None):
    count = in_sems.shape[0]
    slab = part_ref.shape[0] // count
    first = pl.multiple_of((index_ref[THEIRS] * (core_ref.shape[1] // (2 * TILE)) + i) * TILE, TILE)
    staged(
        [part_ref.at[pl.ds(k * slab, slab)] for k in range(count)],
        [stage_ref.at[pl.ds(k * slab, slab)] for k in range(count)],
        [core_ref.at[pl.ds(k * slab, slab), pl.ds(first, TILE), :] for k in range(count)],
        in_sems,
        out_sems,
        meanwhile,
    )


def last_kernel(
    i, index_ref, part_ref, diagonal_ref, cross_ref, old_ref, core_ref, gram_ref, *scratch
):
    stage_ref, in_sems, out_sems, diagonal_stage, cross_stage, pieces_stage, gram_sems = scratch
    z = diagonal_ref.shape[0]
    mine = index_ref[MINE]
    blocks = [pl.ds(pl.multiple_of(at * z, z), z) for at in (mine, 1 - mine)]
    loads = [
        pltpu.make_async_copy(diagonal_ref, diagonal_stage, gram_sems.at[0]),
        pltpu.make_async_copy(cross_ref, pieces_stage, gram_sems.at[1]),
    ]
    stores = [
        pltpu.make_async_copy(diagonal_stage, gram_ref.at[:, blocks[0]], gram_sems.at[2]),
        pltpu.make_async_copy(cross_stage, gram_ref.at[:, blocks[1]], gram_sems.at[3]),
    ]
    for load in loads:
        load.start()
    def gram():
        loads[0].wait()
        stores[0].start()
        loads[1].wait()
        count, high, _ = pieces_stage.shape
        for odd in range(2):
            for t, rows, columns in tiles(count, z // 2, z):
                place = slice(odd * z // 2 + rows.start, odd * z // 2 + rows.stop)
                cross_stage[place, columns] = pieces_stage[t, odd * high // 2 : (odd + 1) * high // 2, :]

        @pl.when(mine == 1)
        def _():
            cross_stage[...] = cross_stage[...].T

        stores[1].start()

    put_kernel(i, index_ref, part_ref, old_ref, core_ref, stage_ref, in_sems, out_sems, gram)
    for store in stores:
        store.wait()


def join_kernel(axis, index_ref, keep_ref, other_ref, out_ref):
    half = keep_ref.shape[axis]
    odd = index_ref[CORE]
    for value_ref, first in ((keep_ref, odd * half), (other_ref, (1 - odd) * half)):
        part = pl.ds(pl.multiple_of(first, half), half)
        out_ref[(part, slice(None)) if axis == 0 else (slice(None), part)] = value_ref[...]


def block_sources(block_owner, block_offset):
    devices = lax.axis_size("xy")
    myself = lax.axis_index("xy")
    owner = lax.dynamic_slice_in_dim(block_owner, myself * BLOCKS_DEV, BLOCKS_DEV)
    offset = lax.dynamic_slice_in_dim(block_offset, myself * BLOCKS_DEV, BLOCKS_DEV)
    lower = (myself + devices - 1) % devices
    source = jnp.where(owner == myself, 0, jnp.where(owner == lower, 1, 2))
    return source.astype(jnp.int32), (offset // POINTS).astype(jnp.int32)


def local_pair(field, factor, block_owner, block_offset):
    z, count, points = field.shape
    mine = lax.axis_index("gz")
    group = count // 2
    rank = factor.shape[1] // 2
    chunks = group // TILE
    columns = points // POINTS
    scale = 1.0 / (count * points * lax.axis_size("xy"))
    source, slot = block_sources(block_owner, block_offset)
    along = lax.axis_index("xy")
    places = jnp.stack([mine, 1 - mine, along % 2]).astype(jnp.int32)
    steps = Steps(jnp.concatenate([places, source, slot]))
    any_space = pl.BlockSpec(memory_space=pl.ANY)
    whole_factor = whole(factor.shape)
    slabs = 4
    axes = ("xy", "gz")

    def staging(rows):
        return [pltpu.VMEM((rows, TILE, points), jnp.float32)] + [pltpu.SemaphoreType.DMA((slabs,))] * 2

    def neighbours(part):
        return part, shifted(part, "xy", 1), shifted(part, "xy", -1)

    def over_gz(part):
        return shifted(part, "gz", 1)

    def exchanged(part, bit):
        return lax.ppermute(part, "xy", [(i, i ^ bit) for i in range(lax.axis_size("xy"))])

    def send_field(i):
        kernel = functools.partial(copy_field_kernel, i)
        out = ((z, TILE, points), any_space)
        index = places if i == 0 else None
        return over_gz(steps.call(kernel, "copy", (1,), [(field, any_space)], [out], None, staging(z), index)[0])

    def send_factor():
        out = ((z, rank), whole((z, rank)))
        half = steps.call(copy_kernel, "copy", (1,), [(factor, ranks(z, rank, CORE))], [out], index=places)[0]
        return over_gz(half)

    def core_send(i, index=None):
        inputs = [(factor, ranks(z, rank, THEIRS)), (field, field_chunk(z, chunks, MINE, i))]
        out = ((rank, TILE, points), core_chunk(rank))
        return steps.call(core_part_kernel, "core_send", (columns,), inputs, [out], index=index)[0]

    def core_finish(i, arrived):
        inputs = [
            (factor, ranks(z, rank, MINE)),
            (field, field_chunk(z, chunks, THEIRS, i)),
            (arrived, core_chunk(rank)),
        ]
        out = ((rank, TILE, points), core_chunk(rank))
        return steps.call(core_finish_kernel, "core_finish", (columns,), inputs, [out])[0]

    def both_halves(i, theirs):
        received = pl.BlockSpec((z, TILE, POINTS), lambda p, w: (0, 0, p))
        return [(field, field_chunk(z, chunks, MINE, i)), (theirs, received)]

    def add_last_cross(i, theirs, cross):
        inputs = both_halves(i, theirs) + [(cross, whole((z, z)))]
        half = ((z // 2, z), whole((z // 2, z)))
        scratch = [pltpu.VMEM((z, z), jnp.float32)]
        return steps.call(cross_last_kernel, "cross", (columns,), inputs, [half, half], None, scratch)

    def core_of(i, theirs, cross_factor, ranks_spec, out_rank):
        inputs = [(factor, ranks_spec), (cross_factor, ranks_spec)] + both_halves(i, theirs)
        out = ((out_rank, TILE, points), core_chunk(out_rank))
        return steps.call(core_kernel, "core", (columns,), inputs, [out])[0]

    def received(i, theirs, cross_factor, cross, ranks_spec, out_rank):
        inputs = [(factor, ranks_spec), (cross_factor, ranks_spec)] + both_halves(i, theirs)
        if cross is not None:
            inputs.append((cross, whole((z, z))))
        outputs = [((out_rank, TILE, points), core_chunk(out_rank)), ((z, z), whole((z, z)))]
        kernel = functools.partial(received_kernel, cross is None)
        return steps.call(kernel, "received", (columns,), inputs, outputs)

    def diagonal_gram():
        block = pl.BlockSpec((z, TILE, POINTS), lambda i, w: (0, i // columns, i % columns))
        scratch = [pltpu.VMEM((z, z), jnp.float32)] * 2
        grid = (count // TILE * columns,)
        half = ((z // 2, z), whole((z // 2, z)))
        kernel = functools.partial(diagonal_kernel, scale)
        return steps.call(kernel, "diagonal", grid, [(field, block)], [half, half], None, scratch)

    def small(kernel, *arrays):
        spec = whole(arrays[0].shape)
        return steps.call(kernel, "small", (1,), [(a, spec) for a in arrays], [(arrays[0].shape, spec)])[0]

    def joined(axis, keep, other):
        spec = whole(keep.shape)
        shape = tuple(n * 2 if k == axis else n for k, n in enumerate(keep.shape))
        kernel = functools.partial(join_kernel, axis)
        return steps.call(kernel, "join", (1,), [(keep, spec), (other, spec)], [(shape, whole(shape))])[0]

    def spread(keep, other):
        shape = (lax.axis_size(axes), z // 2 * z // lax.axis_size(axes) // POINTS, POINTS)
        inputs = [(keep, whole(keep.shape)), (other, whole(other.shape))]
        pieces = steps.call(cut_kernel, "cut", (1,), inputs, [(shape, whole(shape))])[0]
        return lax.all_to_all(pieces, axes, split_axis=0, concat_axis=0, tiled=True)

    def summed(pieces):
        count, high, _ = pieces.shape
        shape = (count, 2 * high, POINTS)
        kernel = functools.partial(sum_kernel, scale)
        total = steps.call(kernel, "sum", (1,), [(pieces, whole(pieces.shape))], [(shape, whole(shape))])[0]
        return lax.all_to_all(total, axes, split_axis=0, concat_axis=0, tiled=True)

    def place(parts, half=None, core=None, at=MINE, i=0):
        rows = (lambda w: 0) if half is None else (lambda w: w[half])
        spec = pl.BlockSpec((rank, TILE, POINTS), lambda j, w: (rows(w), 0, w[SLOT + j]))
        inputs = [(part, spec) for part in parts]
        if core is None:
            out = ((rank, TILE, points), core_chunk(rank))
            return steps.call(place_kernel, "place", (BLOCKS_DEV,), inputs, [out])[0]
        out = ((rank, count, points), field_chunk(rank, chunks, at, i))
        if core is EMPTY:
            return steps.call(place_kernel, "place", (BLOCKS_DEV,), inputs, [out])[0]
        inputs.append((core, any_space))
        return steps.call(place_kernel, "place", (BLOCKS_DEV,), inputs, [out], {3: 0})[0]

    def put(part, core, i):
        out = ((rank, count, points), any_space)
        kernel = functools.partial(put_kernel, i)
        inputs = [(part, any_space), (core, any_space)]
        return steps.call(kernel, "put", (1,), inputs, [out], {1: 0}, staging(rank))[0]

    fields, ready, arrived = {}, {}, {}
    own_ranks = ranks(z, rank, MINE)
    arrived[2] = over_gz(core_send(2, places))
    factor_half = send_factor()
    other_half = exchanged(factor_half, 1)
    fields[0] = send_field(0)
    diagonal, half = diagonal_gram()
    half = exchanged(half, 1)
    fields[1] = send_field(1)
    diagonal = small(add_kernel, diagonal, half)
    half = exchanged(diagonal, 2)
    cross_factor = joined(1, factor_half, other_half)
    late2 = neighbours(core_finish(2, arrived[2]))
    diagonal = small(add_kernel, diagonal, half)
    half = exchanged(diagonal, 4)
    core = place(late2, None, EMPTY, THEIRS, 2)
    diagonal = small(add_kernel, diagonal, half)
    half = exchanged(diagonal, 8)
    part, cross = received(0, fields[0], cross_factor, None, whole_factor, 2 * rank)
    ready[0] = neighbours(part)
    diagonal = small(add_kernel, diagonal, half)
    fields[2] = send_field(2)
    part, cross = received(1, fields[1], cross_factor, cross, whole_factor, 2 * rank)
    ready[1] = neighbours(part)
    core = place(ready[0], MINE, core, MINE, 0)
    fields[3] = send_field(3)
    part, cross = received(2, fields[2], cross_factor, cross, own_ranks, rank)
    ready[2] = neighbours(part)
    core = place(ready[1], MINE, core, MINE, 1)
    diagonal = small(copy_kernel, diagonal)
    half = exchanged(diagonal, 1)
    arrived[3] = over_gz(core_send(3))
    diagonal = joined(0, diagonal, half)
    core = place(ready[2], None, core, MINE, 2)
    ready[3] = neighbours(core_of(3, fields[3], cross_factor, own_ranks, rank))
    keep, send = add_last_cross(3, fields[3], cross)
    half = exchanged(send, 1)
    arrived[0] = over_gz(place(ready[0], THEIRS))
    cross = spread(keep, half)
    arrived[1] = over_gz(place(ready[1], THEIRS))
    late3 = neighbours(core_finish(3, arrived[3]))
    core = place(ready[3], None, core, MINE, 3)
    cross = summed(cross)
    core = put(arrived[0], core, 0)
    core = place(late3, None, core, THEIRS, 3)
    inputs = [(array, any_space) for array in (arrived[1], diagonal, cross, core)]
    outputs = [((rank, count, points), any_space), ((z, 2 * z), any_space)]
    scratch = staging(rank) + [pltpu.VMEM((z, z), jnp.float32)] * 2
    scratch += [pltpu.VMEM(cross.shape, jnp.float32), pltpu.SemaphoreType.DMA((4,))]
    kernel = functools.partial(last_kernel, 1)
    core, gram = steps.call(kernel, "last", (1,), inputs, outputs, {3: 0}, scratch)
    return (gram, core)


EMPTY = object()


def local_many(field, factor, block_owner, block_offset):
    parts = lax.axis_size("gz")
    mine = lax.axis_index("gz")
    z, count, points = field.shape
    scale = 1.0 / (count * points * lax.axis_size("xy"))
    swapped = lax.all_to_all(field, "gz", split_axis=1, concat_axis=0, tiled=True)
    part = jnp.einsum("zcs,wcs->zw", swapped, swapped, precision=lax.Precision.HIGHEST)
    rows = lax.psum_scatter(part, "gz", scatter_dimension=0, tiled=True)
    gram = lax.psum(rows, "xy") * scale
    whole_factor = lax.all_gather(factor, "gz", axis=0, tiled=True)
    core_part = jnp.einsum("zr,zcs->rcs", whole_factor, swapped, precision=lax.Precision.HIGHEST)
    core = lax.all_to_all(core_part, "gz", split_axis=0, concat_axis=1, tiled=True)
    source, slot = block_sources(block_owner, block_offset)
    stack = (core, shifted(core, "xy", 1), shifted(core, "xy", -1))
    blocks = []
    for j in range(BLOCKS_DEV):
        here, lower, upper = (lax.dynamic_slice_in_dim(a, slot[j] * POINTS, POINTS, 2) for a in stack)
        blocks.append(jnp.where(source[j] == 0, here, jnp.where(source[j] == 1, lower, upper)))
    return (gram, jnp.concatenate(blocks, axis=2))


def solution(mesh):
    return jax.shard_map(
        local_pair if mesh.shape["gz"] == 2 else local_many,
        mesh=mesh,
        in_specs=(P("gz", None, "xy"), P("gz", None), P(), P()),
        out_specs=(P("gz", None), P("gz", None, "xy")),
        check_vma=False,
    )
```
